512 devices in a mesh: row: 16 (over z), col: 8 (over y, core), rep: 4 (over x).
Axes of the slice: x: 4, y: 4, z: 16, core: 2. Of those that a mesh axis runs over, the one named last changes fastest.
Arguments:
- p_vals: bfloat16 [384, 16, 128, 128], P('row', 'col'), may hold values from -0.8984375 to 0.8984375
- p_cols: int32 [384, 16], P('row', 'col'), may hold values from 0 to 23
- square_cols: int32 [128, 16, 2], P('row', 'col'), may hold values from 0 to 23, as said below
- cube_cols: int32 [128, 16, 1], P('row', 'col'), may hold values from 0 to 23
Outputs:
- new_density: bfloat16 [128, 16, 1, 128, 128], P(('row', 'rep'), 'col')
The draws below stay inside these ranges and needn't reach their ends.
Inputs may be any that keep to these rules, and one draw needn't show every extreme that they name: `square_cols`: the 2 columns of one block row and group are distinct.
All inputs are finite; a program needn't handle non-finite values.
Results may differ from the reference program's by a relative error of at most 0.014.
Values may be sent and summed in bfloat16 or wider, within the bound.
No kernel may reach another device: no remote copies, remote signals or barrier semaphores. Data moves between devices by JAX's collectives and lax.ppermute only.
A program may use at most 64 MiB of HBM per device.

```python
import jax
import jax.numpy as jnp
from jax import lax

BS = 128
NB = 384
K2 = 2
K3 = 1
WIN = 8
BR = 24
N_ROW = 16
N_REP = 4


def pattern(key):
    return jax.random.randint(jax.random.fold_in(key, 11), (NB, N_ROW), 0, BR).astype(jnp.int32)


def squares(key, base):
    inner_key = jax.random.fold_in(key, 12)
    count = WIN * N_ROW
    order = jnp.arange(count, dtype=jnp.int32)
    upd_rows = order // WIN * BR + order % WIN
    via = jax.random.randint(inner_key, (count, N_ROW, K2), 0, N_ROW).astype(jnp.int32)
    middle = via * BR + base[upd_rows[:, None, None], via]
    groups = jnp.arange(N_ROW, dtype=jnp.int32)[None, :, None]
    cols = base[middle, groups]
    first = cols[:, :, 0]
    second = cols[:, :, 1]
    second = jnp.where(second == first, (second + 1) % BR, second)
    return jnp.stack([first, second], axis=2).astype(jnp.int32)


def draw_p_cols(key, part):
    return pattern(key)


def draw_square_cols(key, part):
    base = pattern(key)
    return squares(key, base)


def draw_cube_cols(key, part):
    base = pattern(key)
    kept = squares(key, base)
    key = jax.random.fold_in(key, 3)
    count = WIN * N_ROW
    pick = jax.random.randint(jax.random.fold_in(key, 1), (count, N_ROW, K3), 0, 2)
    which_group = jax.random.randint(jax.random.fold_in(key, 2), (count, N_ROW, K3), 0, N_ROW).astype(jnp.int32)
    which_slot = jax.random.randint(jax.random.fold_in(key, 4), (count, N_ROW, K3), 0, K2).astype(jnp.int32)
    order = jnp.arange(count, dtype=jnp.int32)[:, None, None]
    inner = which_group * BR + kept[order, which_group, which_slot]
    groups = jnp.arange(N_ROW, dtype=jnp.int32)[None, :, None]
    through = base[inner, groups]
    same = kept[:, :, :1]
    return jnp.where(pick == 0, same, through).astype(jnp.int32)


def level_of(key, dims, cuts, low, largest):
    def one(position, shards_of):
        heights = jax.random.uniform(jax.random.fold_in(jax.random.fold_in(key, 6), position), (shards_of,), jnp.float32, low / len(cuts), largest / len(cuts))
        return jnp.repeat(jnp.exp(heights), dims[position] // shards_of).reshape((-1,) + (1,) * (len(dims) - position - 1))

    level = one(*cuts[0])
    for cut in cuts[1:]:
        level = level * one(*cut)
    return level


def noise(rng, extent, width, bound, shards=(), kind=jnp.bfloat16):
    values = width * jax.random.normal(rng, extent, jnp.float32)
    if shards:
        values = values * level_of(rng, extent, shards, -0.22, 0.18)
    return jnp.clip(values, -bound, bound).astype(kind)


def setup_inputs(seed: int = 0) -> dict:
    seeds = jax.random.split(jax.random.key(seed), 5)
    return {
        "p_vals": noise(seeds[0], (NB, N_ROW, BS, BS), 0.15, 0.8984375, ((0, 16), (1, 8))),
        "p_cols": draw_p_cols(jax.random.fold_in(seeds[4], 71), 0),
        "square_cols": draw_square_cols(jax.random.fold_in(seeds[4], 71), 0),
        "cube_cols": draw_cube_cols(jax.random.fold_in(seeds[4], 71), 0),
    }


def reference(p_vals, p_cols, square_cols, cube_cols):
    count = WIN * N_ROW
    order = jnp.arange(count, dtype=jnp.int32)
    upd_rows = (order // WIN) * BR + order % WIN
    a_vals = p_vals[upd_rows]
    a_cols = p_cols[upd_rows]

    def first_term(s):
        left = lax.dynamic_index_in_dim(a_vals, s, 1, keepdims=False).astype(jnp.float32)
        inner = s * BR + lax.dynamic_index_in_dim(a_cols, s, 1, keepdims=False)
        right = p_vals[inner].astype(jnp.float32)
        right_cols = p_cols[inner]
        match = (square_cols == right_cols[:, :, None]).astype(jnp.float32)
        prod = jnp.einsum('iab,isbc->isac', left, right)
        return match[:, :, :, None, None] * prod[:, :, None]

    square = jnp.zeros((count, N_ROW, K2, BS, BS), jnp.float32)
    for cls in range(N_REP):
        def add_one(q, acc):
            return acc + first_term(q * N_REP + cls)
        part_sum = lax.fori_loop(0, N_ROW // N_REP, add_one, jnp.zeros((count, N_ROW, K2, BS, BS), jnp.float32))
        square = square + part_sum.astype(jnp.bfloat16).astype(jnp.float32)
    square = square.astype(jnp.bfloat16)

    def second_term(s):
        left = lax.dynamic_index_in_dim(square, s, 1, keepdims=False).astype(jnp.float32)
        inner = s * BR + lax.dynamic_index_in_dim(square_cols, s, 1, keepdims=False)
        right = p_vals[inner].astype(jnp.float32)
        right_cols = p_cols[inner]
        match = (right_cols[:, :, :, None] == cube_cols[:, None]).astype(jnp.float32)
        prod = jnp.einsum('itab,itsbc->itsac', left, right)
        return jnp.einsum('itsm,itsac->ismac', match, prod)

    cube = jnp.zeros((count, N_ROW, K3, BS, BS), jnp.float32)
    for cls in range(N_REP):
        def add_two(q, acc):
            return acc + second_term(q * N_REP + cls)
        part_sum = lax.fori_loop(0, N_ROW // N_REP, add_two, jnp.zeros((count, N_ROW, K3, BS, BS), jnp.float32))
        cube = cube + part_sum.astype(jnp.bfloat16).astype(jnp.float32)

    found = (square_cols[:, :, :, None] == cube_cols[:, :, None, :]).astype(jnp.float32)
    at_cube = jnp.einsum('istm,istac->ismac', found, square.astype(jnp.float32))
    return (3.0 * at_cube - 2.0 * cube).astype(jnp.bfloat16)
```

```python
import jax
import jax.numpy as jnp
from jax import lax
from jax.experimental import pallas as pl
from jax.experimental.pallas import tpu as pltpu
from jax.sharding import PartitionSpec as P

ROWS = 16
COLS = 8
REPS = 4
GROUPS = 2
WIN = 8
BR = 24
BS = 128
Q = BS // REPS
HALF = BR + 1
KEPT = 2


def along_row(value, steps):
    pairs = [(i, (i + steps) % ROWS) for i in range(ROWS)]
    return lax.ppermute(value, "row", pairs)


def square_kernel(where, left_cols, cols, keep, lefts, *refs):
    panels, low, high, out, right = refs[:15], refs[15], refs[16], refs[17], refs[18]
    row = where[0]
    lane = lax.broadcasted_iota(jnp.int32, (BS, BS), 1) // Q

    def one(w, _):
        for d in range(ROWS):
            s = lax.rem(row + d, ROWS)
            k = left_cols[w * ROWS + s]
            for g in range(GROUPS):
                if d < 8:
                    block = panels[d][g * HALF + k]
                elif d == 8:
                    block = (low[k], high[1 + k])[g]
                else:
                    block = panels[d - 1][g * HALF + k]
                col = cols[d * GROUPS * BR + g * BR + k]
                for m in range(KEPT):
                    hit = col == keep[w * GROUPS * KEPT + g * KEPT + m]
                    at = (g * KEPT + m) * BS
                    right[pl.ds(pl.multiple_of(s * Q, Q), Q), at : at + BS] = jnp.where(
                        hit, block, jnp.zeros_like(block)
                    )
        full = jnp.dot(lefts[w], right[...], preferred_element_type=jnp.float32)
        parts = [full[:, i * BS : (i + 1) * BS] for i in range(GROUPS * KEPT)]
        for x in range(REPS):
            mixed = parts[x]
            for i in range(GROUPS * KEPT):
                if i != x:
                    moved = pltpu.roll(parts[i], (Q * (i - x)) % BS, 1)
                    mixed = jnp.where(lane == i, moved, mixed)
            out[x, w] = mixed.astype(jnp.bfloat16)
        return 0

    lax.fori_loop(0, WIN, one, 0)


def cube_kernel(where, mid_cols, cols, keep, own_keep, lefts, own, *refs):
    panels, low, high, out, right = refs[:15], refs[15], refs[16], refs[17], refs[18]
    row, rep = where[0], where[1]
    inner = ROWS * KEPT * Q
    wide = lax.broadcasted_iota(jnp.int32, (BS, BS), 1)
    tall = lax.broadcasted_iota(jnp.int32, (BS, BS), 0)
    place = wide == (rep * Q + tall % Q)
    slot = tall // Q

    def one(w, _):
        for d in range(ROWS):
            s = lax.rem(row + d, ROWS)
            for t in range(KEPT):
                k = mid_cols[w * ROWS * KEPT + s * KEPT + t]
                for g in range(GROUPS):
                    if d < 8:
                        block = panels[d][g * HALF + k]
                    elif d == 8:
                        block = (low[k], high[1 + k])[g]
                    else:
                        block = panels[d - 1][g * HALF + k]
                    hit = cols[d * GROUPS * BR + g * BR + k] == keep[w * GROUPS + g]
                    at = pl.multiple_of((s * KEPT + t) * Q, Q)
                    right[pl.ds(at, Q), g * BS : (g + 1) * BS] = jnp.where(
                        hit, block, jnp.zeros_like(block)
                    )
        for g in range(GROUPS):
            found = jnp.zeros((BS, BS), jnp.float32)
            for m in range(KEPT):
                hit = own_keep[w * GROUPS * KEPT + g * KEPT + m] == keep[w * GROUPS + g]
                scale = jnp.where(hit, -1.5, 0.0)
                found = jnp.where(slot == g * KEPT + m, scale, found)
            found = jnp.where(place, found, 0.0)
            right[inner : inner + BS, g * BS : (g + 1) * BS] = found.astype(jnp.bfloat16)
        total = jnp.dot(own[w], right[inner : inner + BS, :], preferred_element_type=jnp.float32)
        for c in range(COLS):
            total += jnp.dot(
                lefts[c, w], right[c * BS : (c + 1) * BS, :], preferred_element_type=jnp.float32
            )
        total = -2.0 * total
        for g in range(GROUPS):
            out[w, g] = total[:, g * BS : (g + 1) * BS].astype(jnp.bfloat16)
        return 0

    lax.fori_loop(0, WIN, one, 0)


def on_device(p_vals, p_cols, square_cols, cube_cols):
    row = lax.axis_index("row")
    rep = lax.axis_index("rep")
    smem = pl.BlockSpec(memory_space=pltpu.SMEM)
    vmem = pl.BlockSpec(memory_space=pltpu.VMEM)

    mine = lax.dynamic_slice_in_dim(p_vals, rep * Q, Q, 2)
    marks = p_cols.T.reshape(1, 1, GROUPS * BR).astype(jnp.bfloat16)
    marks = jnp.pad(marks, ((0, 0), (0, Q - 1), (0, BS - GROUPS * BR)))
    panel = jnp.concatenate([mine[:, 0], marks, mine[:, 1]], axis=0)

    left = lax.dynamic_slice_in_dim(p_vals[:WIN], rep * Q, Q, 3)
    left = left.transpose(0, 2, 1, 3).reshape(WIN // 2, 2, BS, GROUPS * Q)
    left = left.transpose(0, 2, 1, 3).reshape(WIN // 2 * BS, BS)
    notes = jnp.concatenate([p_cols[:WIN].reshape(-1), square_cols.reshape(-1)])
    notes = jnp.pad(notes.astype(jnp.bfloat16)[None], ((0, 15), (0, BS - notes.shape[0])))
    lefts = lax.all_gather(jnp.concatenate([left, notes], axis=0), "col")
    notes = lefts[:, WIN // 2 * BS, :].astype(jnp.int32)
    left_cols = notes[:, : WIN * GROUPS].reshape(COLS, WIN, GROUPS).transpose(1, 0, 2).reshape(-1)
    mid_cols = notes[:, WIN * GROUPS : WIN * GROUPS * (1 + KEPT)]
    mid_cols = mid_cols.reshape(COLS, WIN, GROUPS, KEPT).transpose(1, 0, 2, 3).reshape(-1)
    lefts = lefts[:, : WIN // 2 * BS].reshape(COLS, WIN // 2, BS, 2, GROUPS * Q)
    lefts = lefts.transpose(1, 3, 2, 0, 4).reshape(WIN, BS, ROWS * Q)

    ups, downs = [panel], [panel]
    for _ in range(ROWS // 2 - 1):
        ups.append(along_row(ups[-1], 1))
        downs.append(along_row(downs[-1], -1))
    low = along_row(ups[-1][:HALF], 1)
    high = along_row(downs[-1][HALF - 1 :], -1)
    panels = downs + ups[:0:-1]
    marks = [p[BR, 0, : GROUPS * BR] for p in panels]
    marks.insert(8, low[BR, 0, : GROUPS * BR])
    cols = jnp.concatenate(marks).astype(jnp.int32)

    where = jnp.stack([row, rep]).astype(jnp.int32)
    keep = square_cols.reshape(-1)
    partial = pl.pallas_call(
        square_kernel,
        out_shape=jax.ShapeDtypeStruct((REPS, WIN, BS, BS), jnp.bfloat16),
        in_specs=[smem] * 4 + [vmem] * 18,
        out_specs=vmem,
        scratch_shapes=[pltpu.VMEM((ROWS * Q, GROUPS * KEPT * BS), jnp.bfloat16)],
        compiler_params=pltpu.CompilerParams(vmem_limit_bytes=40 * 2**20),
    )(where, left_cols, cols, keep, lefts, *panels, low, high)
    parts = lax.all_to_all(partial, "rep", 0, 0, tiled=True)
    own = jnp.sum(parts.astype(jnp.float32), axis=0).astype(jnp.bfloat16)
    squares = lax.all_to_all(jnp.broadcast_to(own[None], (COLS,) + own.shape), "col", 0, 0)
    partial = pl.pallas_call(
        cube_kernel,
        out_shape=jax.ShapeDtypeStruct((WIN, GROUPS, BS, BS), jnp.bfloat16),
        in_specs=[smem] * 5 + [vmem] * 19,
        out_specs=vmem,
        scratch_shapes=[pltpu.VMEM((ROWS * KEPT * Q + BS, GROUPS * BS), jnp.bfloat16)],
        compiler_params=pltpu.CompilerParams(vmem_limit_bytes=40 * 2**20),
    )(where, mid_cols, cols, cube_cols.reshape(-1), keep, squares, own, *panels, low, high)
    parts = lax.all_to_all(partial, "rep", 0, 0, tiled=True)
    parts = parts.reshape((REPS, WIN // REPS) + parts.shape[1:]).astype(jnp.float32)
    return jnp.sum(parts, axis=0).astype(jnp.bfloat16)[:, :, None]


def solution(mesh):
    in_specs = (
        P("row", "col", None, None),
        P("row", "col"),
        P("row", "col", None),
        P("row", "col", None),
    )
    out_specs = P(("row", "rep"), "col", None, None, None)
    return jax.shard_map(
        on_device, mesh=mesh, in_specs=in_specs, out_specs=out_specs, check_vma=False
    )
```

```python
import jax
import jax.numpy as jnp
from jax import lax
from jax.experimental import pallas as pl
from jax.experimental.pallas import tpu as pltpu
from jax.sharding import PartitionSpec as P

ROWS = 16
COLS = 8
CHIPS = 4
REPS = 4
GROUPS = 2
WIN = 8
BR = 24
BS = 128
Q = BS // REPS
HALF = BR + 1
KEPT = 2
SLOTS = GROUPS * KEPT
MARKS = GROUPS * BR
INNER = ROWS * KEPT * Q

EVEN = [(i, i ^ 1) for i in range(ROWS)]
ODD = [(i, (i + 1) % ROWS if i % 2 else (i - 1) % ROWS) for i in range(ROWS)]
CORES = [(i, i ^ 1) for i in range(COLS)]
SAME_CORE = [[c + i for i in range(0, COLS, 2)] for c in range(2)]

SMEM = pl.BlockSpec(memory_space=pltpu.SMEM)
VMEM = pl.BlockSpec(memory_space=pltpu.VMEM)


def over_even(value):
    return lax.ppermute(value, "row", EVEN)


def over_odd(value):
    return lax.ppermute(value, "row", ODD)


def step_of(where, offset):
    return lax.rem(where[0] + where[2] * offset + ROWS, ROWS)


def put_square(right, w, s, blocks, cols, base, k, keep):
    for g in range(GROUPS):
        block = blocks[g]
        col = cols[base + g * BR + k]
        for m in range(KEPT):
            slot = g * KEPT + m
            hit = col == keep[w * SLOTS + slot]
            right[w, pl.ds(pl.multiple_of(s * Q, Q), Q), slot * BS : (slot + 1) * BS] = jnp.where(
                hit, block, jnp.zeros_like(block)
            )


def put_cube(right, w, s, t, blocks, cols, base, k, keep):
    at = pl.multiple_of((s * KEPT + t) * Q, Q)
    for g in range(GROUPS):
        block = blocks[g]
        hit = cols[base + g * BR + k] == keep[w * GROUPS + g]
        right[w, pl.ds(at, Q), g * BS : (g + 1) * BS] = jnp.where(hit, block, jnp.zeros_like(block))


def late_blocks(i, k, near, far, low, high):
    if i < 2:
        panel = (near, far)[i]
        return panel[k], panel[HALF + k]
    return low[k], high[1 + k]


LATE = (ROWS // 2 - 1, 1 - ROWS // 2, ROWS // 2)


def early_kernel(where, left_cols, mid_cols, cols, keep, cube_keep, *refs):
    panels, squares, cubes = refs[:-2], refs[-2], refs[-1]
    wide = lax.broadcasted_iota(jnp.int32, (BS, BS), 1)
    tall = lax.broadcasted_iota(jnp.int32, (BS, BS), 0)
    place = wide == (where[1] * Q + tall % Q)
    near = (len(panels) + 1) // 2

    def one(w, _):
        for i, panel in enumerate(panels):
            s = step_of(where, i if i < near else near - 1 - i)
            k = left_cols[w * ROWS + s]
            put_square(squares, w, s, (panel[k], panel[HALF + k]), cols, i * MARKS, k, keep)
            for t in range(KEPT):
                k = mid_cols[(w * ROWS + s) * KEPT + t]
                blocks = (panel[k], panel[HALF + k])
                put_cube(cubes, w, s, t, blocks, cols, i * MARKS, k, cube_keep)
        for g in range(GROUPS):
            found = jnp.zeros((BS, BS), jnp.float32)
            for m in range(KEPT):
                hit = keep[w * SLOTS + g * KEPT + m] == cube_keep[w * GROUPS + g]
                scale = jnp.where(hit, -1.5, 0.0)
                found = jnp.where(tall // Q == g * KEPT + m, scale, found)
            found = jnp.where(place, found, 0.0)
            cubes[w, INNER : INNER + BS, g * BS : (g + 1) * BS] = found.astype(jnp.bfloat16)
        return 0

    lax.fori_loop(0, WIN, one, 0)


def square_kernel(where, left_cols, cols, keep, lefts, near, far, low, high, given, out, right):
    lane = lax.broadcasted_iota(jnp.int32, (BS, BS), 1) // Q

    def one(w, _):
        for i, offset in enumerate(LATE):
            s = step_of(where, offset)
            k = left_cols[w * ROWS + s]
            blocks = late_blocks(i, k, near, far, low, high)
            put_square(right, w, s, blocks, cols, i * MARKS, k, keep)
        rows = pl.ds(pl.multiple_of(w * BS, BS), BS)
        left = jnp.concatenate([lefts[y, rows, :] for y in range(CHIPS)], axis=1)
        full = jnp.dot(left, right[w], preferred_element_type=jnp.float32)
        parts = [full[:, i * BS : (i + 1) * BS] for i in range(SLOTS)]
        for x in range(REPS):
            mixed = parts[x]
            for i in range(SLOTS):
                if i != x:
                    moved = pltpu.roll(parts[i], (Q * (i - x)) % BS, 1)
                    mixed = jnp.where(lane == i, moved, mixed)
            out[x, w] = mixed.astype(jnp.bfloat16)
        return 0

    lax.fori_loop(0, WIN, one, 0)


def late_kernel(where, mid_cols, cols, cube_keep, near, far, low, high, given, right):
    def one(w, _):
        for i, offset in enumerate(LATE):
            s = step_of(where, offset)
            for t in range(KEPT):
                k = mid_cols[(w * ROWS + s) * KEPT + t]
                blocks = late_blocks(i, k, near, far, low, high)
                put_cube(right, w, s, t, blocks, cols, i * MARKS, k, cube_keep)
        return 0

    lax.fori_loop(0, WIN, one, 0)


def cube_kernel(where, own, same, other, right, out):
    core = where[3]

    def one(w, _):
        total = jnp.dot(own[w], right[w, INNER:, :], preferred_element_type=jnp.float32)
        for y in range(CHIPS):
            for lefts, c in ((same, 2 * y + core), (other, 2 * y + 1 - core)):
                rows = pl.ds(pl.multiple_of(c * BS, BS), BS)
                total += jnp.dot(lefts[y, w], right[w, rows, :], preferred_element_type=jnp.float32)
        total = -2.0 * total
        for g in range(GROUPS):
            out[w, g] = total[:, g * BS : (g + 1) * BS].astype(jnp.bfloat16)
        return 0

    lax.fori_loop(0, WIN, one, 0)


def call(kernel, out, scalars, arrays, aliases=None, flops=0):
    moved = sum(a.size * 2 for a in arrays)
    return pl.pallas_call(
        kernel,
        out_shape=out,
        in_specs=[SMEM] * len(scalars) + [VMEM] * len(arrays),
        out_specs=jax.tree.map(lambda _: VMEM, out),
        input_output_aliases=aliases or {},
        cost_estimate=pl.CostEstimate(flops=flops, bytes_accessed=moved, transcendentals=0),
        compiler_params=pltpu.CompilerParams(vmem_limit_bytes=8 * 2**20),
    )(*scalars, *arrays)


def shaped(*shape):
    return jax.ShapeDtypeStruct(shape, jnp.bfloat16)


def columns_of(marks):
    return jnp.concatenate([m[BR, 0, :MARKS] for m in marks]).astype(jnp.int32)


def on_device(p_vals, p_cols, square_cols, cube_cols):
    row = lax.axis_index("row")
    rep = lax.axis_index("rep")
    core = lax.axis_index("col") % 2
    where = jnp.stack([row, rep, 1 - 2 * (row % 2), core]).astype(jnp.int32)

    mine = lax.dynamic_slice_in_dim(p_vals, rep * Q, Q, 2)
    marks = p_cols.T.reshape(1, 1, MARKS).astype(jnp.bfloat16)
    marks = jnp.pad(marks, ((0, 0), (0, Q - 1), (0, BS - MARKS)))
    panel = jnp.concatenate([mine[:, 0], marks, mine[:, 1]], axis=0)

    left = lax.dynamic_slice_in_dim(p_vals[:WIN], rep * Q, Q, 3)
    left = left.transpose(0, 2, 1, 3).reshape(WIN * BS, GROUPS * Q)
    notes = jnp.concatenate([p_cols[:WIN].reshape(-1), square_cols.reshape(-1)])
    notes = jnp.pad(notes.astype(jnp.bfloat16)[None], ((0, 15), (0, GROUPS * Q - notes.shape[0])))
    left = jnp.concatenate([left, notes], axis=0)
    beside = lax.ppermute(left, "col", CORES)
    left = jnp.where(
        core == 0,
        jnp.concatenate([left, beside], axis=1),
        jnp.concatenate([beside, left], axis=1),
    )
    lefts = lax.all_gather(left, "col", axis_index_groups=SAME_CORE)
    notes = lefts[:, WIN * BS, :].astype(jnp.int32).reshape(COLS, GROUPS * Q)
    left_cols = notes[:, : WIN * GROUPS].reshape(COLS, WIN, GROUPS).transpose(1, 0, 2).reshape(-1)
    mid_cols = notes[:, WIN * GROUPS : WIN * GROUPS * (1 + KEPT)]
    mid_cols = mid_cols.reshape(COLS, WIN, GROUPS, KEPT).transpose(1, 0, 2, 3).reshape(-1)

    evens, odds = [panel], [panel]
    for _ in range(ROWS // 2 - 1):
        even, odd = over_even(odds[-1]), over_odd(evens[-1])
        evens.append(even)
        odds.append(odd)
    low = over_even(odds[-1][:HALF])
    high = over_odd(evens[-1][HALF - 1 :])
    early = evens[:-1] + odds[1:-1]
    late = [evens[-1], odds[-1], low, high]

    keep = square_cols.reshape(-1)
    cube_keep = cube_cols.reshape(-1)
    squares, cubes = call(
        early_kernel,
        (shaped(WIN, ROWS * Q, SLOTS * BS), shaped(WIN, INNER + BS, GROUPS * BS)),
        (where, left_cols, mid_cols, columns_of(early), keep, cube_keep),
        early,
    )
    cols = columns_of(late[:3])
    partial, _ = call(
        square_kernel,
        (shaped(REPS, WIN, BS, BS), shaped(*squares.shape)),
        (where, left_cols, cols, keep),
        (lefts, *late, squares),
        {9: 1},
        WIN * 2 * BS * ROWS * Q * SLOTS * BS,
    )
    cubes = call(late_kernel, shaped(*cubes.shape), (where, mid_cols, cols, cube_keep), (*late, cubes), {8: 0})
    parts = lax.all_to_all(partial, "rep", 0, 0, tiled=True)
    own = jnp.sum(parts.astype(jnp.float32), axis=0).astype(jnp.bfloat16)
    same = lax.all_to_all(
        jnp.broadcast_to(own[None], (CHIPS,) + own.shape), "col", 0, 0, axis_index_groups=SAME_CORE
    )
    other = lax.ppermute(same, "col", CORES)
    partial = call(
        cube_kernel,
        shaped(WIN, GROUPS, BS, BS),
        (where,),
        (own, same, other, cubes),
        None,
        WIN * 2 * BS * (INNER + BS) * GROUPS * BS,
    )
    parts = lax.all_to_all(partial, "rep", 0, 0, tiled=True)
    parts = parts.reshape((REPS, WIN // REPS) + parts.shape[1:]).astype(jnp.float32)
    return jnp.sum(parts, axis=0).astype(jnp.bfloat16)[:, :, None]


def solution(mesh):
    in_specs = (
        P("row", "col", None, None),
        P("row", "col"),
        P("row", "col", None),
        P("row", "col", None),
    )
    out_specs = P(("row", "rep"), "col", None, None, None)
    return jax.shard_map(
        on_device, mesh=mesh, in_specs=in_specs, out_specs=out_specs, check_vma=False
    )
```

```python
import jax
import jax.numpy as jnp
from jax import lax
from jax.experimental import pallas as pl
from jax.experimental.pallas import tpu as pltpu
from jax.sharding import PartitionSpec as P

ROWS = 16
COLS = 8
CHIPS = 4
REPS = 4
GROUPS = 2
WIN = 8
BR = 24
BS = 128
Q = BS // REPS
HALF = BR + 1
KEPT = 2
SLOTS = GROUPS * KEPT
MARKS = GROUPS * BR
INNER = ROWS * KEPT * Q

CORES = [(i, i ^ 1) for i in range(COLS)]
SAME_CORE = [[c + i for i in range(0, COLS, 2)] for c in range(2)]

SMEM = pl.BlockSpec(memory_space=pltpu.SMEM)
VMEM = pl.BlockSpec(memory_space=pltpu.VMEM)


def put(right, w, at, n, block, hit):
    at = at if isinstance(at, int) else pl.multiple_of(at, Q)
    right[w, pl.ds(at, Q), n * BS : (n + 1) * BS] = jnp.where(hit, block, jnp.zeros_like(block))


def square_kernel(left_cols, cols, keep, lefts, panels, out, right):
    lane = lax.broadcasted_iota(jnp.int32, (BS, BS), 1) // Q
    right[...] = jnp.zeros_like(right)

    def pair(p, _):
        rows = pl.ds(pl.multiple_of(p * BS, BS), BS)
        left = jnp.concatenate([lefts[c, rows, :] for c in range(COLS)], axis=1)
        for half in range(2):
            w = 2 * p + half
            for s in range(ROWS):
                k = left_cols[w * ROWS + s]
                at = (s // GROUPS) * BS + (half * GROUPS + s % GROUPS) * Q
                for g in range(GROUPS):
                    block = panels[s, g * HALF + k]
                    col = cols[s * MARKS + g * BR + k]
                    for m in range(KEPT):
                        slot = g * KEPT + m
                        put(right, half, at, slot, block, col == keep[w * SLOTS + slot])
            full = jnp.dot(left, right[half], preferred_element_type=jnp.float32)
            parts = [full[:, i * BS : (i + 1) * BS] for i in range(SLOTS)]
            for x in range(REPS):
                mixed = parts[x]
                for i in range(SLOTS):
                    if i != x:
                        moved = pltpu.roll(parts[i], (Q * (i - x)) % BS, 1)
                        mixed = jnp.where(lane == i, moved, mixed)
                out[x, w] = mixed.astype(jnp.bfloat16)
        return 0

    lax.fori_loop(0, WIN // 2, pair, 0)


def cube_kernel(where, mid_cols, cols, keep, cube_keep, own, same, other, panels, out, right):
    rep, core = where[0], where[1]
    wide = lax.broadcasted_iota(jnp.int32, (BS, BS), 1)
    tall = lax.broadcasted_iota(jnp.int32, (BS, BS), 0)
    place = wide == (rep * Q + tall % Q)

    def pair(p, _):
        for half in range(2):
            w = 2 * p + half
            for s in range(ROWS):
                for t in range(KEPT):
                    k = mid_cols[(w * ROWS + s) * KEPT + t]
                    for g in range(GROUPS):
                        hit = cols[s * MARKS + g * BR + k] == cube_keep[w * GROUPS + g]
                        put(right, half, (s * KEPT + t) * Q, g, panels[s, g * HALF + k], hit)
            for g in range(GROUPS):
                found = jnp.zeros((BS, BS), jnp.float32)
                for m in range(KEPT):
                    hit = keep[w * SLOTS + g * KEPT + m] == cube_keep[w * GROUPS + g]
                    found = jnp.where(tall // Q == g * KEPT + m, jnp.where(hit, -1.5, 0.0), found)
                found = jnp.where(place, found, 0.0).astype(jnp.bfloat16)
                right[half, INNER : INNER + BS, g * BS : (g + 1) * BS] = found
            total = jnp.dot(own[w], right[half, INNER:, :], preferred_element_type=jnp.float32)
            for y in range(CHIPS):
                for lefts, c in ((same, 2 * y + core), (other, 2 * y + 1 - core)):
                    rows = pl.ds(pl.multiple_of(c * BS, BS), BS)
                    total += jnp.dot(
                        lefts[y, w], right[half, rows, :], preferred_element_type=jnp.float32
                    )
            total = -2.0 * total
            for g in range(GROUPS):
                out[w, g] = total[:, g * BS : (g + 1) * BS].astype(jnp.bfloat16)
        return 0

    lax.fori_loop(0, WIN // 2, pair, 0)


def call(kernel, out, scalars, arrays, scratch, flops):
    moved = sum(a.size * 2 for a in arrays)
    return pl.pallas_call(
        kernel,
        out_shape=jax.ShapeDtypeStruct(out, jnp.bfloat16),
        in_specs=[SMEM] * len(scalars) + [VMEM] * len(arrays),
        out_specs=VMEM,
        scratch_shapes=[pltpu.VMEM(scratch, jnp.bfloat16)],
        cost_estimate=pl.CostEstimate(flops=flops, bytes_accessed=moved, transcendentals=0),
        compiler_params=pltpu.CompilerParams(vmem_limit_bytes=8 * 2**20),
    )(*scalars, *arrays)


def on_device(p_vals, p_cols, square_cols, cube_cols):
    rep = lax.axis_index("rep")
    core = lax.axis_index("col") % 2
    where = jnp.stack([rep, core]).astype(jnp.int32)

    left = lax.dynamic_slice_in_dim(p_vals[:WIN], rep * Q, Q, 3)
    left = left.reshape(WIN // 2, 2, GROUPS, BS, Q).transpose(0, 3, 1, 2, 4)
    left = left.reshape(WIN // 2 * BS, BS)
    notes = jnp.concatenate([p_cols[:WIN].reshape(-1), square_cols.reshape(-1)])
    notes = jnp.pad(notes.astype(jnp.bfloat16)[None], ((0, 15), (0, BS - notes.shape[0])))
    lefts = lax.all_gather(jnp.concatenate([left, notes], axis=0), "col")
    notes = lefts[:, WIN // 2 * BS, :].astype(jnp.int32)
    left_cols = notes[:, : WIN * GROUPS].reshape(COLS, WIN, GROUPS).transpose(1, 0, 2).reshape(-1)
    mid_cols = notes[:, WIN * GROUPS : WIN * GROUPS * (1 + KEPT)]
    mid_cols = mid_cols.reshape(COLS, WIN, GROUPS, KEPT).transpose(1, 0, 2, 3).reshape(-1)

    mine = lax.dynamic_slice_in_dim(p_vals, rep * Q, Q, 2)
    peak = jnp.max(jnp.abs(mine)).astype(jnp.float32)
    power = jnp.clip(13.0 - jnp.floor(jnp.log2(jnp.maximum(peak, 1e-37))), 0.0, 110.0)
    mine = (mine.astype(jnp.float32) * jnp.exp2(power)).astype(jnp.float16)
    marks = jnp.concatenate([p_cols.T.reshape(-1).astype(jnp.float32), power[None]])
    marks = marks.astype(jnp.float16)[None, None]
    marks = jnp.pad(marks, ((0, 0), (0, Q - 1), (0, BS - MARKS - 1)))
    panels = lax.all_gather(jnp.concatenate([mine[:, 0], marks, mine[:, 1]], axis=0), "row")
    marks = panels[:, BR, 0, : MARKS + 1].astype(jnp.float32)
    cols = marks[:, :MARKS].astype(jnp.int32).reshape(-1)
    back = jnp.exp2(-marks[:, MARKS])[:, None, None, None]
    panels = (panels.astype(jnp.float32) * back).astype(jnp.bfloat16)

    keep = square_cols.reshape(-1)
    partial = call(
        square_kernel,
        (REPS, WIN, BS, BS),
        (left_cols, cols, keep),
        (lefts, panels),
        (2, COLS * BS, SLOTS * BS),
        WIN * 2 * BS * COLS * BS * SLOTS * BS,
    )
    parts = lax.all_to_all(partial, "rep", 0, 0, tiled=True)
    own = jnp.sum(parts.astype(jnp.float32), axis=0).astype(jnp.bfloat16)
    same = lax.all_to_all(
        jnp.broadcast_to(own[None], (CHIPS,) + own.shape), "col", 0, 0, axis_index_groups=SAME_CORE
    )
    other = lax.ppermute(same, "col", CORES)
    partial = call(
        cube_kernel,
        (WIN, GROUPS, BS, BS),
        (where, mid_cols, cols, keep, cube_cols.reshape(-1)),
        (own, same, other, panels),
        (2, INNER + BS, GROUPS * BS),
        WIN * 2 * BS * (INNER + BS) * GROUPS * BS,
    )
    parts = lax.all_to_all(partial, "rep", 0, 0, tiled=True)
    parts = parts.reshape((REPS, WIN // REPS) + parts.shape[1:]).astype(jnp.float32)
    return jnp.sum(parts, axis=0).astype(jnp.bfloat16)[:, :, None]


def solution(mesh):
    in_specs = (
        P("row", "col", None, None),
        P("row", "col"),
        P("row", "col", None),
        P("row", "col", None),
    )
    out_specs = P(("row", "rep"), "col", None, None, None)
    return jax.shard_map(
        on_device, mesh=mesh, in_specs=in_specs, out_specs=out_specs, check_vma=False
    )
```

```python
import jax
import jax.numpy as jnp
from jax import lax
from jax.experimental import pallas as pl
from jax.experimental.pallas import tpu as pltpu
from jax.sharding import PartitionSpec as P

ROWS = 16
COLS = 8
CHIPS = 4
REPS = 4
GROUPS = 2
WIN = 8
BR = 24
BS = 128
Q = BS // REPS
HALF = BR + 1
KEPT = 2
SLOTS = GROUPS * KEPT
MARKS = GROUPS * BR
ROOM = 48
INNER = ROWS * KEPT * Q

CORES = [(i, i ^ 1) for i in range(COLS)]
SAME_CORE = [[c + i for i in range(0, COLS, 2)] for c in range(2)]

SMEM = pl.BlockSpec(memory_space=pltpu.SMEM)
HBM = pl.BlockSpec(memory_space=pltpu.HBM)
VMEM = pl.BlockSpec(memory_space=pltpu.VMEM)


def put(right, w, at, n, block, hit):
    at = at if isinstance(at, int) else pl.multiple_of(at, Q)
    right[w, pl.ds(at, Q), n * BS : (n + 1) * BS] = jnp.where(hit, block, jnp.zeros_like(block))


def fetch(panels, held, sems):
    copies = [pltpu.make_async_copy(panels.at[s], held.at[s], sems.at[s]) for s in range(ROWS)]
    for copy in copies:
        copy.start()
    return copies


def prepare_kernel(where, p_cols, square_cols, p_vals, spread, panel, heads, shares, sems):
    rep = where[0]
    rows = pl.ds(pl.multiple_of(rep * Q, Q), Q)
    first = pltpu.make_async_copy(p_vals.at[:WIN], heads, sems.at[0])
    second = pltpu.make_async_copy(p_vals.at[:, :, rows, :], shares, sems.at[1])
    first.start()
    second.start()
    lane = lax.broadcasted_iota(jnp.int32, (2 * 8, BS), 1)
    notes = jnp.zeros((2 * 8, BS), jnp.float32)
    for i in range(WIN * GROUPS):
        notes = jnp.where(lane == i, p_cols[i].astype(jnp.float32), notes)
    for i in range(WIN * SLOTS):
        notes = jnp.where(lane == WIN * GROUPS + i, square_cols[i].astype(jnp.float32), notes)
    notes = notes.astype(jnp.bfloat16)
    marks = jnp.zeros((2 * 8, BS), jnp.float32)
    for g in range(GROUPS):
        for k in range(BR):
            marks = jnp.where(lane == g * BR + k, p_cols[k * GROUPS + g].astype(jnp.float32), marks)

    group = lax.broadcasted_iota(jnp.int32, (BS, BS), 1) // Q
    first.wait()
    for p in range(WIN // 2):
        tile = jnp.zeros((BS, BS), jnp.float32)
        for i in range(2 * GROUPS):
            part = heads[2 * p + i // GROUPS, i % GROUPS].astype(jnp.float32)
            moved = pltpu.roll(part, lax.rem((i - rep) * Q + BS, BS), 1)
            tile = jnp.where(group == i, moved, tile)
        tile = tile.astype(jnp.bfloat16)
        for c in range(COLS):
            spread[c, p * BS : (p + 1) * BS, :] = tile
    for c in range(COLS):
        spread[c, WIN // 2 * BS :, :] = notes

    second.wait()
    peak = jnp.zeros((Q, BS), jnp.float32)
    for k in range(BR):
        for g in range(GROUPS):
            block = shares[k, g]
            panel[g * HALF + k] = block
            peak = jnp.maximum(peak, jnp.abs(block.astype(jnp.float32)))
    peak = jnp.maximum(jnp.max(peak, axis=(0, 1), keepdims=True), 1e-37)
    power = jnp.clip(13.0 - jnp.floor(jnp.log2(peak)), 0.0, 110.0)
    marks = jnp.where(lane == MARKS, power, marks)
    panel[BR] = jnp.concatenate([marks, marks], axis=0).astype(jnp.bfloat16)


def square_kernel(left_cols, cols, keep, lefts, panels, out, held, left, right, sems):
    copies = fetch(panels, held, sems)
    lane = lax.broadcasted_iota(jnp.int32, (BS, BS), 1)

    def gather_left(p, _):
        rows = pl.ds(pl.multiple_of(p * BS, BS), BS)
        for c in range(0, COLS, 2):
            one, two = lefts[c, rows, :].astype(jnp.float32), lefts[c + 1, rows, :].astype(jnp.float32)
            low = jnp.where(lane < BS // 2, one, pltpu.roll(two, BS // 2, 1))
            high = jnp.where(lane < BS // 2, pltpu.roll(one, BS // 2, 1), two)
            left[2 * p, :, c * BS // 2 : (c + 2) * BS // 2] = low.astype(jnp.bfloat16)
            left[2 * p + 1, :, c * BS // 2 : (c + 2) * BS // 2] = high.astype(jnp.bfloat16)
        return 0

    lax.fori_loop(0, WIN // 2, gather_left, 0)
    for s in range(ROWS):
        copies[s].wait()

        def one(w, _):
            k = left_cols[w * ROWS + s]
            for g in range(GROUPS):
                block = held[s, g * HALF + k]
                col = cols[s * MARKS + g * BR + k]
                for m in range(KEPT):
                    slot = g * KEPT + m
                    put(right, w, s * Q, slot, block, col == keep[w * SLOTS + slot])
            return 0

        lax.fori_loop(0, WIN, one, 0, unroll=True)

    def multiply(w, _):
        full = jnp.dot(left[w], right[w], preferred_element_type=jnp.float32)
        parts = [full[:, i * BS : (i + 1) * BS] for i in range(SLOTS)]
        for x in range(REPS):
            mixed = parts[x]
            for i in range(SLOTS):
                if i != x:
                    moved = pltpu.roll(parts[i], (Q * (i - x)) % BS, 1)
                    mixed = jnp.where(lane // Q == i, moved, mixed)
            out[x, w] = mixed.astype(jnp.bfloat16)
        return 0

    lax.fori_loop(0, WIN, multiply, 0)


def layout_kernel(where, mid_cols, cols, keep, cube_keep, panels, right, held, sems):
    copies = fetch(panels, held, sems)
    rep = where[0]
    wide = lax.broadcasted_iota(jnp.int32, (BS, BS), 1)
    tall = lax.broadcasted_iota(jnp.int32, (BS, BS), 0)
    place = wide == (rep * Q + tall % Q)

    def own(w, _):
        for g in range(GROUPS):
            found = jnp.zeros((BS, BS), jnp.float32)
            for m in range(KEPT):
                hit = keep[w * SLOTS + g * KEPT + m] == cube_keep[w * GROUPS + g]
                found = jnp.where(tall // Q == g * KEPT + m, jnp.where(hit, -1.5, 0.0), found)
            found = jnp.where(place, found, 0.0).astype(jnp.bfloat16)
            right[w, INNER : INNER + BS, g * BS : (g + 1) * BS] = found
        return 0

    lax.fori_loop(0, WIN, own, 0)
    for s in range(ROWS):
        copies[s].wait()

        def one(w, _):
            for t in range(KEPT):
                k = mid_cols[(w * ROWS + s) * KEPT + t]
                for g in range(GROUPS):
                    hit = cols[s * MARKS + g * BR + k] == cube_keep[w * GROUPS + g]
                    put(right, w, (s * KEPT + t) * Q, g, held[s, g * HALF + k], hit)
            return 0

        lax.fori_loop(0, WIN, one, 0, unroll=True)


def cube_kernel(where, own, same, other, right, out):
    core = where[1]

    def one(w, _):
        total = jnp.dot(own[w], right[w, INNER:, :], preferred_element_type=jnp.float32)
        for y in range(CHIPS):
            for lefts, c in ((same, 2 * y + core), (other, 2 * y + 1 - core)):
                rows = pl.ds(pl.multiple_of(c * BS, BS), BS)
                total += jnp.dot(lefts[y, w], right[w, rows, :], preferred_element_type=jnp.float32)
        total = -2.0 * total
        for g in range(GROUPS):
            out[w, g] = total[:, g * BS : (g + 1) * BS].astype(jnp.bfloat16)
        return 0

    lax.fori_loop(0, WIN, one, 0)


def shaped(*shape):
    return jax.ShapeDtypeStruct(shape, jnp.bfloat16)


def call(kernel, out, scalars, arrays, scratch=(), specs=None, room=8, work=(0, 0)):
    return pl.pallas_call(
        kernel,
        out_shape=out,
        in_specs=[SMEM] * len(scalars) + (specs or [VMEM] * len(arrays)),
        out_specs=jax.tree.map(lambda _: VMEM, out),
        scratch_shapes=scratch,
        cost_estimate=pl.CostEstimate(flops=work[0], bytes_accessed=work[1], transcendentals=0),
        compiler_params=pltpu.CompilerParams(vmem_limit_bytes=room * 2**20),
    )(*scalars, *arrays)


def on_device(p_vals, p_cols, square_cols, cube_cols):
    rep = lax.axis_index("rep")
    core = lax.axis_index("col") % 2
    where = jnp.stack([rep, core]).astype(jnp.int32)
    keep = square_cols.reshape(-1)
    cube_keep = cube_cols.reshape(-1)

    spread, panel = call(
        prepare_kernel,
        (shaped(COLS, WIN // 2 * BS + 16, BS), shaped(GROUPS * BR + 1, Q, BS)),
        (where, p_cols.reshape(-1), keep),
        [p_vals],
        [
            pltpu.VMEM((WIN, GROUPS, BS, BS), jnp.bfloat16),
            pltpu.VMEM((BR, GROUPS, Q, BS), jnp.bfloat16),
            pltpu.SemaphoreType.DMA((2,)),
        ],
        [HBM],
        63,
    )
    lefts = lax.all_to_all(spread, "col", 0, 0)
    scale = jnp.exp2(panel[BR, 0, MARKS].astype(jnp.float32))
    plain = lax.broadcasted_iota(jnp.int32, panel.shape, 0) == BR
    panel = (panel.astype(jnp.float32) * jnp.where(plain, 1.0, scale)).astype(jnp.float16)
    panels = lax.all_gather(panel, "row")
    panels, lefts = lax.optimization_barrier((panels, lefts))
    notes = lefts[:, WIN // 2 * BS, :].astype(jnp.int32)
    left_cols = notes[:, : WIN * GROUPS].reshape(COLS, WIN, GROUPS).transpose(1, 0, 2).reshape(-1)
    mid_cols = notes[:, WIN * GROUPS : WIN * GROUPS * (1 + KEPT)]
    mid_cols = mid_cols.reshape(COLS, WIN, GROUPS, KEPT).transpose(1, 0, 2, 3).reshape(-1)
    marks = panels[:, BR, 0, : MARKS + 1].astype(jnp.float32)
    cols = marks[:, :MARKS].astype(jnp.int32).reshape(-1)
    back = jnp.exp2(-marks[:, MARKS])[:, None, None, None]
    panels = (panels.astype(jnp.float32) * back).astype(jnp.bfloat16)
    held = [pltpu.VMEM(panels.shape, panels.dtype)]
    sems = [pltpu.SemaphoreType.DMA((ROWS,))]

    partial = call(
        square_kernel,
        shaped(REPS, WIN, BS, BS),
        (left_cols, cols, keep),
        (lefts, panels),
        held
        + [
            pltpu.VMEM((WIN, BS, ROWS * Q), jnp.bfloat16),
            pltpu.VMEM((WIN, ROWS * Q, SLOTS * BS), jnp.bfloat16),
        ]
        + sems,
        [VMEM, HBM],
        ROOM,
        (WIN * 2 * BS * ROWS * Q * SLOTS * BS, panels.size * 2),
    )
    right = call(
        layout_kernel,
        shaped(WIN, INNER + BS, GROUPS * BS),
        (where, mid_cols, cols, keep, cube_keep),
        [panels],
        held + sems,
        [HBM],
        ROOM,
        (0, 3 * panels.size * 2),
    )
    parts = lax.all_to_all(partial, "rep", 0, 0, tiled=True)
    own = jnp.sum(parts.astype(jnp.float32), axis=0).astype(jnp.bfloat16)
    same = lax.all_to_all(
        jnp.broadcast_to(own[None], (CHIPS,) + own.shape), "col", 0, 0, axis_index_groups=SAME_CORE
    )
    other = lax.ppermute(same, "col", CORES)
    partial = call(
        cube_kernel,
        shaped(WIN, GROUPS, BS, BS),
        (where,),
        (own, same, other, right),
        work=(WIN * 2 * BS * (INNER + BS) * GROUPS * BS, right.size * 2),
    )
    parts = lax.all_to_all(partial, "rep", 0, 0, tiled=True)
    parts = parts.reshape((REPS, WIN // REPS) + parts.shape[1:]).astype(jnp.float32)
    return jnp.sum(parts, axis=0).astype(jnp.bfloat16)[:, :, None]


def solution(mesh):
    in_specs = (
        P("row", "col", None, None),
        P("row", "col"),
        P("row", "col", None),
        P("row", "col", None),
    )
    out_specs = P(("row", "rep"), "col", None, None, None)
    return jax.shard_map(
        on_device, mesh=mesh, in_specs=in_specs, out_specs=out_specs, check_vma=False
    )
```

```python
import jax
import jax.numpy as jnp
from jax import lax
from jax.experimental import pallas as pl
from jax.experimental.pallas import tpu as pltpu
from jax.sharding import PartitionSpec as P

ROWS = 16
COLS = 8
CHIPS = 4
REPS = 4
GROUPS = 2
WIN = 8
BR = 24
BS = 128
Q = BS // REPS
HALF = BR + 1
KEPT = 2
SLOTS = GROUPS * KEPT
MARKS = GROUPS * BR
ROOM = 48
INNER = ROWS * KEPT * Q

CORES = [(i, i ^ 1) for i in range(COLS)]
SAME_CORE = [[c + i for i in range(0, COLS, 2)] for c in range(2)]

SMEM = pl.BlockSpec(memory_space=pltpu.SMEM)
HBM = pl.BlockSpec(memory_space=pltpu.HBM)
VMEM = pl.BlockSpec(memory_space=pltpu.VMEM)


def put(right, w, row, lane_tile, block, hit, spare):
    row = pl.multiple_of(jnp.where(hit, row, spare), Q)
    right[w, pl.ds(row, Q), pl.ds(pl.multiple_of(lane_tile * BS, BS), BS)] = block


def clear(right, rows):
    def one(w, _):
        right[w, :rows, :] = jnp.zeros((rows, right.shape[2]), right.dtype)
        return 0

    lax.fori_loop(0, WIN, one, 0)


def fetch(panels, held, sems):
    copies = [pltpu.make_async_copy(panels.at[s], held.at[s], sems.at[s]) for s in range(ROWS)]
    for copy in copies:
        copy.start()
    return copies


def prepare_kernel(p_cols, square_cols, p_vals, spread, panel, heads, shares, sems):
    rep = lax.axis_index("rep")
    rows = pl.ds(pl.multiple_of(rep * Q, Q), Q)
    first = pltpu.make_async_copy(p_vals.at[:WIN], heads, sems.at[0])
    second = pltpu.make_async_copy(p_vals.at[:, :, rows, :], shares, sems.at[1])
    first.start()
    second.start()
    lane = lax.broadcasted_iota(jnp.int32, (2 * 8, BS), 1)
    notes = jnp.zeros((2 * 8, BS), jnp.float32)
    for w in range(WIN):
        for g in range(GROUPS):
            at = w * GROUPS + g
            notes = jnp.where(lane == at, p_cols[g, w].astype(jnp.float32), notes)
            for m in range(KEPT):
                value = square_cols[g, m, w].astype(jnp.float32)
                notes = jnp.where(lane == WIN * GROUPS + at * KEPT + m, value, notes)
    notes = notes.astype(jnp.bfloat16)
    marks = jnp.zeros((2 * 8, BS), jnp.float32)
    for g in range(GROUPS):
        for k in range(BR):
            marks = jnp.where(lane == g * BR + k, p_cols[g, k].astype(jnp.float32), marks)

    group = lax.broadcasted_iota(jnp.int32, (BS, BS), 1) // Q
    first.wait()
    for p in range(WIN // 2):
        tile = jnp.zeros((BS, BS), jnp.float32)
        for i in range(2 * GROUPS):
            part = heads[2 * p + i // GROUPS, i % GROUPS].astype(jnp.float32)
            moved = pltpu.roll(part, lax.rem((i - rep) * Q + BS, BS), 1)
            tile = jnp.where(group == i, moved, tile)
        tile = tile.astype(jnp.bfloat16)
        for c in range(COLS):
            spread[c, p * BS : (p + 1) * BS, :] = tile
    for c in range(COLS):
        spread[c, WIN // 2 * BS :, :] = notes

    second.wait()
    peak = jnp.zeros((Q, BS), jnp.float32)
    for k in range(BR):
        for g in range(GROUPS):
            peak = jnp.maximum(peak, jnp.abs(shares[k, g].astype(jnp.float32)))
    peak = jnp.maximum(jnp.max(peak, axis=(0, 1), keepdims=True), 1e-37)
    power = jnp.clip(13.0 - jnp.floor(jnp.log2(peak)), 0.0, 110.0)
    scale = jnp.exp2(power)
    for k in range(BR):
        for g in range(GROUPS):
            block = shares[k, g].astype(jnp.float32) * scale
            panel[g * HALF + k] = block.astype(jnp.bfloat16)
    marks = jnp.where(lane == MARKS, power, marks)
    panel[BR] = jnp.concatenate([marks, marks], axis=0).astype(jnp.bfloat16)


def square_kernel(notes, marks, keep, lefts, panels, out, right, held, sems):
    def pick(p):
        for half in range(2):
            for s in range(ROWS):
                k = notes[s // GROUPS, 0, (2 * p + half) * GROUPS + s % GROUPS]
                for g in range(GROUPS):
                    pltpu.make_async_copy(
                        panels.at[s, g * HALF + k], held.at[p, half, s, g], sems.at[p]
                    ).start()

    pick(0)
    group = lax.broadcasted_iota(jnp.int32, (BS, BS), 1) // Q
    right[...] = jnp.zeros_like(right)

    def pair(p, _):
        @pl.when(p < WIN // 2 - 1)
        def _():
            pick(p + 1)

        pltpu.make_async_copy(held.at[p], held.at[p], sems.at[p]).wait()
        rows = pl.ds(pl.multiple_of(p * BS, BS), BS)
        left = jnp.concatenate([lefts[c, rows, :] for c in range(COLS)], axis=1)
        for half in range(2):
            w = 2 * p + half
            for s in range(ROWS):
                k = notes[s // GROUPS, 0, w * GROUPS + s % GROUPS]
                at = (s // GROUPS) * BS + (half * GROUPS + s % GROUPS) * Q
                for g in range(GROUPS):
                    block = held[p, half, s, g]
                    col = marks[s, g * BR + k]
                    for m in range(KEPT):
                        n = (g * KEPT + m) * BS
                        right[half, at : at + Q, n : n + BS] = jnp.where(
                            col == keep[g, m, w], block, jnp.zeros_like(block)
                        )
            full = jnp.dot(left, right[half], preferred_element_type=jnp.float32)
            p4 = [full[:, i * BS : (i + 1) * BS] for i in range(SLOTS)]
            u = [jnp.where(group < 2, p4[i], pltpu.roll(p4[i + 2], BS // 2, 1)) for i in range(2)]
            u += [jnp.where(group < 2, pltpu.roll(p4[i], BS // 2, 1), p4[i + 2]) for i in range(2)]
            for i in (0, 2):
                one = jnp.where(group % 2 == 0, u[i], pltpu.roll(u[i + 1], Q, 1))
                two = jnp.where(group % 2 == 0, pltpu.roll(u[i], BS - Q, 1), u[i + 1])
                out[i, w] = one.astype(jnp.bfloat16)
                out[i + 1, w] = two.astype(jnp.bfloat16)
        return 0

    lax.fori_loop(0, WIN // 2, pair, 0)


def layout_kernel(notes, marks, keep, cube_keep, panels, right, held, sems):
    copies = fetch(panels, held, sems)
    clear(right, INNER)
    rep = lax.axis_index("rep")
    wide = lax.broadcasted_iota(jnp.int32, (BS, BS), 1)
    tall = lax.broadcasted_iota(jnp.int32, (BS, BS), 0)
    place = wide == (rep * Q + tall % Q)

    def own(w, _):
        for g in range(GROUPS):
            found = jnp.zeros((BS, BS), jnp.float32)
            for m in range(KEPT):
                scale = jnp.where(keep[g, m, w] == cube_keep[g, 0, w], -1.5, 0.0)
                found = jnp.where(tall // Q == g * KEPT + m, scale, found)
            found = jnp.where(place, found, 0.0).astype(jnp.bfloat16)
            right[w, INNER : INNER + BS, g * BS : (g + 1) * BS] = found
        return 0

    lax.fori_loop(0, WIN, own, 0)
    for s in range(ROWS):
        copies[s].wait()
        for w in range(WIN):
            for t in range(KEPT):
                at = WIN * GROUPS + (w * GROUPS + s % GROUPS) * KEPT + t
                k = notes[s // GROUPS, 0, at]
                for g in range(GROUPS):
                    hit = marks[s, g * BR + k] == cube_keep[g, 0, w]
                    row = (s * KEPT + t) * Q
                    put(right, w, row, g, held[s, g * HALF + k], hit, INNER + BS)


def cube_kernel(own, same, other, right, out):
    core = lax.rem(lax.axis_index("col"), 2)

    def one(w, _):
        total = jnp.dot(own[w], right[w, INNER : INNER + BS, :], preferred_element_type=jnp.float32)
        for y in range(CHIPS):
            for lefts, c in ((same, 2 * y + core), (other, 2 * y + 1 - core)):
                rows = pl.ds(pl.multiple_of(c * BS, BS), BS)
                total += jnp.dot(lefts[y, w], right[w, rows, :], preferred_element_type=jnp.float32)
        total = -2.0 * total
        for g in range(GROUPS):
            out[w, g] = total[:, g * BS : (g + 1) * BS].astype(jnp.bfloat16)
        return 0

    lax.fori_loop(0, WIN, one, 0)


def shaped(*shape):
    return jax.ShapeDtypeStruct(shape, jnp.bfloat16)


def call(kernel, out, scalars, arrays, scratch=(), specs=None, room=8, work=(0, 0)):
    return pl.pallas_call(
        kernel,
        out_shape=out,
        in_specs=[SMEM] * len(scalars) + (specs or [VMEM] * len(arrays)),
        out_specs=jax.tree.map(lambda _: VMEM, out),
        scratch_shapes=scratch,
        cost_estimate=pl.CostEstimate(flops=work[0], bytes_accessed=work[1], transcendentals=0),
        compiler_params=pltpu.CompilerParams(vmem_limit_bytes=room * 2**20),
    )(*scalars, *arrays)


def on_device(p_vals, p_cols, square_cols, cube_cols):
    own_cols = p_cols.T
    keep = square_cols.transpose(1, 2, 0)
    cube_keep = cube_cols.transpose(1, 2, 0)

    spread, panel = call(
        prepare_kernel,
        (shaped(COLS, WIN // 2 * BS + 16, BS), shaped(GROUPS * BR + 1, Q, BS)),
        (own_cols, keep),
        [p_vals],
        [
            pltpu.VMEM((WIN, GROUPS, BS, BS), jnp.bfloat16),
            pltpu.VMEM((BR, GROUPS, Q, BS), jnp.bfloat16),
            pltpu.SemaphoreType.DMA((2,)),
        ],
        [HBM],
        63,
    )
    lefts = lax.all_to_all(spread, "col", 0, 0)
    panels = lax.all_gather(panel.astype(jnp.float16), "row")
    panels = lax.optimization_barrier(panels)
    notes = lefts[:, WIN // 2 * BS : WIN // 2 * BS + 1, :].astype(jnp.int32)
    marks = panels[:, BR, 0, :].astype(jnp.float32)
    back = jnp.exp2(-marks[:, MARKS])[:, None, None, None]
    marks = marks.astype(jnp.int32)
    panels = (panels.astype(jnp.float32) * back).astype(jnp.bfloat16)

    partial = call(
        square_kernel,
        shaped(REPS, WIN, BS, BS),
        (notes, marks, keep),
        (lefts, panels),
        [
            pltpu.VMEM((2, COLS * BS, SLOTS * BS), jnp.bfloat16),
            pltpu.VMEM((WIN // 2, 2, ROWS, GROUPS, Q, BS), jnp.bfloat16),
            pltpu.SemaphoreType.DMA((WIN // 2,)),
        ],
        [VMEM, HBM],
        ROOM,
        (WIN * 2 * BS * ROWS * Q * SLOTS * BS, panels.size * 2),
    )
    right = call(
        layout_kernel,
        shaped(WIN, INNER + BS + Q, GROUPS * BS),
        (notes, marks, keep, cube_keep),
        [panels],
        [pltpu.VMEM(panels.shape, panels.dtype), pltpu.SemaphoreType.DMA((ROWS,))],
        [HBM],
        ROOM,
        (0, 3 * panels.size * 2),
    )
    parts = lax.all_to_all(partial, "rep", 0, 0, tiled=True)
    own = jnp.sum(parts.astype(jnp.float32), axis=0).astype(jnp.bfloat16)
    same = lax.all_to_all(
        jnp.broadcast_to(own[None], (CHIPS,) + own.shape), "col", 0, 0, axis_index_groups=SAME_CORE
    )
    other = lax.ppermute(same, "col", CORES)
    partial = call(
        cube_kernel,
        shaped(WIN, GROUPS, BS, BS),
        (),
        (own, same, other, right),
        work=(WIN * 2 * BS * (INNER + BS) * GROUPS * BS, right.size * 2),
    )
    parts = lax.all_to_all(partial, "rep", 0, 0, tiled=True)
    parts = parts.reshape((REPS, WIN // REPS) + parts.shape[1:]).astype(jnp.float32)
    return jnp.sum(parts, axis=0).astype(jnp.bfloat16)[:, :, None]


def solution(mesh):
    in_specs = (
        P("row", "col", None, None),
        P("row", "col"),
        P("row", "col", None),
        P("row", "col", None),
    )
    out_specs = P(("row", "rep"), "col", None, None, None)
    return jax.shard_map(
        on_device, mesh=mesh, in_specs=in_specs, out_specs=out_specs, check_vma=False
    )
```

```python
import jax
import jax.numpy as jnp
from jax import lax
from jax.experimental import pallas as pl
from jax.experimental.pallas import tpu as pltpu
from jax.sharding import PartitionSpec as P

ROWS = 16
COLS = 8
CHIPS = 4
REPS = 4
GROUPS = 2
WIN = 8
BR = 24
BS = 128
Q = BS // REPS
KEPT = 2
SLOTS = GROUPS * KEPT
MARKS = GROUPS * BR
ROOM = 48
INNER = ROWS * KEPT * Q
PAIR = GROUPS * Q
TALL = BR * PAIR + 16

CORES = [(i, i ^ 1) for i in range(COLS)]
SAME_CORE = [[c + i for i in range(0, COLS, 2)] for c in range(2)]

SMEM = pl.BlockSpec(memory_space=pltpu.SMEM)
HBM = pl.BlockSpec(memory_space=pltpu.HBM)
VMEM = pl.BlockSpec(memory_space=pltpu.VMEM)


def put(right, w, row, lane_tile, block, hit, spare):
    row = pl.multiple_of(jnp.where(hit, row, spare), Q)
    right[w, pl.ds(row, Q), pl.ds(pl.multiple_of(lane_tile * BS, BS), BS)] = block


def clear(right, rows):
    def one(w, _):
        right[w, :rows, :] = jnp.zeros((rows, right.shape[2]), right.dtype)
        return 0

    lax.fori_loop(0, WIN, one, 0)


def scalars(sources, held, sems):
    copies = [pltpu.make_async_copy(*pair, sems.at[i]) for i, pair in enumerate(zip(sources, held))]
    for copy in copies:
        copy.start()
    return copies


def fetch(panels, held, sems):
    copies = [pltpu.make_async_copy(panels.at[s], held.at[s], sems.at[s]) for s in range(ROWS)]
    for copy in copies:
        copy.start()
    return copies


def prepare_kernel(p_cols_in, square_in, p_vals, spread, panel, heads, shares, sems, *small):
    p_cols, square_cols, small_sems = small
    rep = lax.axis_index("rep")
    rows = pl.ds(pl.multiple_of(rep * Q, Q), Q)
    first = pltpu.make_async_copy(p_vals.at[:WIN], heads, sems.at[0])
    second = pltpu.make_async_copy(p_vals.at[:, :, rows, :], shares, sems.at[1])
    first.start()
    second.start()
    for copy in scalars((p_cols_in, square_in), (p_cols, square_cols), small_sems):
        copy.wait()
    lane = lax.broadcasted_iota(jnp.int32, (2 * 8, BS), 1)
    notes = jnp.zeros((2 * 8, BS), jnp.float32)
    for w in range(WIN):
        for g in range(GROUPS):
            at = w * GROUPS + g
            notes = jnp.where(lane == at, p_cols[g, w].astype(jnp.float32), notes)
            for m in range(KEPT):
                value = square_cols[g, m, w].astype(jnp.float32)
                notes = jnp.where(lane == WIN * GROUPS + at * KEPT + m, value, notes)
    notes = notes.astype(jnp.bfloat16)
    marks = jnp.zeros((2 * 8, BS), jnp.float32)
    for g in range(GROUPS):
        for k in range(BR):
            marks = jnp.where(lane == g * BR + k, p_cols[g, k].astype(jnp.float32), marks)

    group = lax.broadcasted_iota(jnp.int32, (BS, BS), 1) // Q
    first.wait()
    for p in range(WIN // 2):
        tile = jnp.zeros((BS, BS), jnp.float32)
        for i in range(2 * GROUPS):
            part = heads[2 * p + i // GROUPS, i % GROUPS].astype(jnp.float32)
            moved = pltpu.roll(part, lax.rem((i - rep) * Q + BS, BS), 1)
            tile = jnp.where(group == i, moved, tile)
        tile = tile.astype(jnp.bfloat16)
        for c in range(COLS):
            spread[c, p * BS : (p + 1) * BS, :] = tile
    for c in range(COLS):
        spread[c, WIN // 2 * BS :, :] = notes

    second.wait()
    peak = jnp.zeros((Q, BS), jnp.float32)
    for k in range(BR):
        for g in range(GROUPS):
            peak = jnp.maximum(peak, jnp.abs(shares[k, g].astype(jnp.float32)))
    peak = jnp.maximum(jnp.max(peak, axis=(0, 1), keepdims=True), 1e-37)
    power = jnp.clip(13.0 - jnp.floor(jnp.log2(peak)), 0.0, 110.0)
    scale = jnp.exp2(power)
    for k in range(BR):
        for g in range(GROUPS):
            block = shares[k, g].astype(jnp.float32) * scale
            panel[k * PAIR + g * Q : k * PAIR + (g + 1) * Q, :] = block.astype(jnp.bfloat16)
    marks = jnp.where(lane == MARKS, power, marks)
    panel[BR * PAIR :, :] = marks.astype(jnp.bfloat16)


def square_kernel(notes_in, marks_in, keep_in, lefts, panels, out, right, held, sems, *small):
    notes, marks, keep, small_sems = small
    waits = scalars((notes_in, marks_in, keep_in), small[:-1], small_sems)

    def pick(p):
        for half in range(2):
            for s in range(ROWS):
                k = notes[s // GROUPS, 0, (2 * p + half) * GROUPS + s % GROUPS]
                rows = pl.ds(pl.multiple_of(k * PAIR, PAIR), PAIR)
                pltpu.make_async_copy(
                    panels.at[s, rows, :], held.at[p, half, s], sems.at[p]
                ).start()

    waits[0].wait()
    pick(0)
    group = lax.broadcasted_iota(jnp.int32, (BS, BS), 1) // Q
    right[...] = jnp.zeros_like(right)
    for copy in waits[1:]:
        copy.wait()

    def pair(p, _):
        if p < WIN // 2 - 1:
            pick(p + 1)

        pltpu.make_async_copy(held.at[p], held.at[p], sems.at[p]).wait()
        rows = pl.ds(pl.multiple_of(p * BS, BS), BS)
        left = jnp.concatenate([lefts[c, rows, :] for c in range(COLS)], axis=1)
        for half in range(2):
            w = 2 * p + half
            for s in range(ROWS):
                k = notes[s // GROUPS, 0, w * GROUPS + s % GROUPS]
                at = (s // GROUPS) * BS + (half * GROUPS + s % GROUPS) * Q
                for g in range(GROUPS):
                    block = held[p, half, s, g * Q : (g + 1) * Q, :]
                    col = marks[s, g * BR + k]
                    for m in range(KEPT):
                        n = (g * KEPT + m) * BS
                        right[half, at : at + Q, n : n + BS] = jnp.where(
                            col == keep[g, m, w], block, jnp.zeros_like(block)
                        )
            full = jnp.dot(left, right[half], preferred_element_type=jnp.float32)
            p4 = [full[:, i * BS : (i + 1) * BS] for i in range(SLOTS)]
            u = [jnp.where(group < 2, p4[i], pltpu.roll(p4[i + 2], BS // 2, 1)) for i in range(2)]
            u += [jnp.where(group < 2, pltpu.roll(p4[i], BS // 2, 1), p4[i + 2]) for i in range(2)]
            for i in (0, 2):
                one = jnp.where(group % 2 == 0, u[i], pltpu.roll(u[i + 1], Q, 1))
                two = jnp.where(group % 2 == 0, pltpu.roll(u[i], BS - Q, 1), u[i + 1])
                out[i, w] = one.astype(jnp.bfloat16)
                out[i + 1, w] = two.astype(jnp.bfloat16)
        return 0

    for p in range(WIN // 2):
        pair(p, 0)


def layout_kernel(notes_in, marks_in, keep_in, cube_keep_in, panels, right, held, sems, *small):
    notes, marks, keep, cube_keep, small_sems = small
    sources = (notes_in, marks_in, keep_in, cube_keep_in)
    waits = scalars(sources, small[:-1], small_sems)
    copies = fetch(panels, held, sems)
    clear(right, INNER)
    for copy in waits:
        copy.wait()
    rep = lax.axis_index("rep")
    wide = lax.broadcasted_iota(jnp.int32, (BS, BS), 1)
    tall = lax.broadcasted_iota(jnp.int32, (BS, BS), 0)
    place = wide == (rep * Q + tall % Q)

    def own(w, _):
        for g in range(GROUPS):
            found = jnp.zeros((BS, BS), jnp.float32)
            for m in range(KEPT):
                scale = jnp.where(keep[g, m, w] == cube_keep[g, 0, w], -1.5, 0.0)
                found = jnp.where(tall // Q == g * KEPT + m, scale, found)
            found = jnp.where(place, found, 0.0).astype(jnp.bfloat16)
            right[w, INNER : INNER + BS, g * BS : (g + 1) * BS] = found
        return 0

    lax.fori_loop(0, WIN, own, 0)
    for s in range(ROWS):
        copies[s].wait()
        for w in range(WIN):
            for t in range(KEPT):
                at = WIN * GROUPS + (w * GROUPS + s % GROUPS) * KEPT + t
                k = notes[s // GROUPS, 0, at]
                for g in range(GROUPS):
                    hit = marks[s, g * BR + k] == cube_keep[g, 0, w]
                    row = (s * KEPT + t) * Q
                    block = held[s, pl.ds(pl.multiple_of(k * PAIR + g * Q, Q), Q), :]
                    put(right, w, row, g, block, hit, INNER + BS)


def cube_kernel(own, same, other, right, out):
    core = lax.rem(lax.axis_index("col"), 2)

    def one(w, _):
        total = jnp.dot(own[w], right[w, INNER : INNER + BS, :], preferred_element_type=jnp.float32)
        for y in range(CHIPS):
            for lefts, c in ((same, 2 * y + core), (other, 2 * y + 1 - core)):
                rows = pl.ds(pl.multiple_of(c * BS, BS), BS)
                total += jnp.dot(lefts[y, w], right[w, rows, :], preferred_element_type=jnp.float32)
        total = -2.0 * total
        for g in range(GROUPS):
            out[w, g] = total[:, g * BS : (g + 1) * BS].astype(jnp.bfloat16)
        return 0

    lax.fori_loop(0, WIN, one, 0)


def small_room(*arrays):
    held = [pltpu.SMEM(a.shape, a.dtype) for a in arrays]
    return (*held, pltpu.SemaphoreType.DMA((len(arrays),)))


def shaped(*shape):
    return jax.ShapeDtypeStruct(shape, jnp.bfloat16)


def call(kernel, out, scalars, arrays, scratch=(), specs=None, room=8, work=(0, 0)):
    return pl.pallas_call(
        kernel,
        out_shape=out,
        in_specs=[SMEM] * len(scalars) + (specs or [VMEM] * len(arrays)),
        out_specs=jax.tree.map(lambda _: VMEM, out),
        scratch_shapes=scratch,
        cost_estimate=pl.CostEstimate(flops=work[0], bytes_accessed=work[1], transcendentals=0),
        compiler_params=pltpu.CompilerParams(vmem_limit_bytes=room * 2**20),
    )(*scalars, *arrays)


def on_device(p_vals, p_cols, square_cols, cube_cols):
    own_cols = p_cols.T
    keep = square_cols.transpose(1, 2, 0)
    cube_keep = cube_cols.transpose(1, 2, 0)

    spread, panel = call(
        prepare_kernel,
        (shaped(COLS, WIN // 2 * BS + 16, BS), shaped(TALL, BS)),
        (),
        [own_cols, keep, p_vals],
        [
            pltpu.VMEM((WIN, GROUPS, BS, BS), jnp.bfloat16),
            pltpu.VMEM((BR, GROUPS, Q, BS), jnp.bfloat16),
            pltpu.SemaphoreType.DMA((2,)),
            *small_room(own_cols, keep),
        ],
        [HBM] * 3,
        63,
    )
    lefts = lax.all_to_all(spread, "col", 0, 0)
    panels = lax.all_gather(panel.astype(jnp.float16), "row")
    panels = lax.optimization_barrier(panels)
    notes = lefts[:, WIN // 2 * BS : WIN // 2 * BS + 1, :].astype(jnp.int32)
    marks = panels[:, BR * PAIR, :].astype(jnp.float32)
    back = jnp.exp2(-marks[:, MARKS])[:, None, None]
    marks = marks.astype(jnp.int32)
    panels = (panels.astype(jnp.float32) * back).astype(jnp.bfloat16)

    partial = call(
        square_kernel,
        shaped(REPS, WIN, BS, BS),
        (),
        (notes, marks, keep, lefts, panels),
        [
            pltpu.VMEM((2, COLS * BS, SLOTS * BS), jnp.bfloat16),
            pltpu.VMEM((WIN // 2, 2, ROWS, PAIR, BS), jnp.bfloat16),
            pltpu.SemaphoreType.DMA((WIN // 2,)),
            *small_room(notes, marks, keep),
        ],
        [HBM] * 3 + [VMEM, HBM],
        ROOM,
        (WIN * 2 * BS * ROWS * Q * SLOTS * BS, panels.size * 2),
    )
    right = call(
        layout_kernel,
        shaped(WIN, INNER + BS + Q, GROUPS * BS),
        (),
        [notes, marks, keep, cube_keep, panels],
        [
            pltpu.VMEM(panels.shape, panels.dtype),
            pltpu.SemaphoreType.DMA((ROWS,)),
            *small_room(notes, marks, keep, cube_keep),
        ],
        [HBM] * 5,
        ROOM,
        (0, 3 * panels.size * 2),
    )
    parts = lax.all_to_all(partial, "rep", 0, 0, tiled=True)
    own = jnp.sum(parts.astype(jnp.float32), axis=0).astype(jnp.bfloat16)
    same = lax.all_to_all(
        jnp.broadcast_to(own[None], (CHIPS,) + own.shape), "col", 0, 0, axis_index_groups=SAME_CORE
    )
    other = lax.ppermute(same, "col", CORES)
    partial = call(
        cube_kernel,
        shaped(WIN, GROUPS, BS, BS),
        (),
        (own, same, other, right),
        work=(WIN * 2 * BS * (INNER + BS) * GROUPS * BS, right.size * 2),
    )
    parts = lax.all_to_all(partial, "rep", 0, 0, tiled=True)
    parts = parts.reshape((REPS, WIN // REPS) + parts.shape[1:]).astype(jnp.float32)
    return jnp.sum(parts, axis=0).astype(jnp.bfloat16)[:, :, None]


def solution(mesh):
    in_specs = (
        P("row", "col", None, None),
        P("row", "col"),
        P("row", "col", None),
        P("row", "col", None),
    )
    out_specs = P(("row", "rep"), "col", None, None, None)
    return jax.shard_map(
        on_device, mesh=mesh, in_specs=in_specs, out_specs=out_specs, check_vma=False
    )
```

```python
import jax
import jax.numpy as jnp
from jax import lax
from jax.experimental import pallas as pl
from jax.experimental.pallas import tpu as pltpu
from jax.sharding import PartitionSpec as P

ROWS = 16
COLS = 8
CHIPS = 4
REPS = 4
GROUPS = 2
WIN = 8
BR = 24
BS = 128
Q = BS // REPS
KEPT = 2
SLOTS = GROUPS * KEPT
MARKS = GROUPS * BR
ROOM = 48
INNER = ROWS * KEPT * Q
PAIR = GROUPS * Q
TALL = BR * PAIR + 16

CORES = [(i, i ^ 1) for i in range(COLS)]
SAME_CORE = [[c + i for i in range(0, COLS, 2)] for c in range(2)]

SMEM = pl.BlockSpec(memory_space=pltpu.SMEM)
HBM = pl.BlockSpec(memory_space=pltpu.HBM)
VMEM = pl.BlockSpec(memory_space=pltpu.VMEM)


def put(right, w, row, lane_tile, block, hit, spare):
    row = pl.multiple_of(jnp.where(hit, row, spare), Q)
    right[w, pl.ds(row, Q), pl.ds(pl.multiple_of(lane_tile * BS, BS), BS)] = block


def clear(right, rows):
    def one(w, _):
        right[w, :rows, :] = jnp.zeros((rows, right.shape[2]), right.dtype)
        return 0

    lax.fori_loop(0, WIN, one, 0)


def scalars(sources, held, sems):
    copies = [pltpu.make_async_copy(*pair, sems.at[i]) for i, pair in enumerate(zip(sources, held))]
    for copy in copies:
        copy.start()
    return copies


def fetch(panels, held, sems):
    copies = [pltpu.make_async_copy(panels.at[s], held.at[s], sems.at[s]) for s in range(ROWS)]
    for copy in copies:
        copy.start()
    return copies


def prepare_kernel(p_cols_in, square_in, p_vals, spread, panel, heads, shares, sems, *small):
    p_cols, square_cols, small_sems = small
    rep = lax.axis_index("rep")
    rows = pl.ds(pl.multiple_of(rep * Q, Q), Q)
    first = pltpu.make_async_copy(p_vals.at[:WIN], heads, sems.at[0])
    second = pltpu.make_async_copy(p_vals.at[:, :, rows, :], shares, sems.at[1])
    first.start()
    second.start()
    for copy in scalars((p_cols_in, square_in), (p_cols, square_cols), small_sems):
        copy.wait()
    lane = lax.broadcasted_iota(jnp.int32, (2 * 8, BS), 1)
    notes = jnp.zeros((2 * 8, BS), jnp.float32)
    for w in range(WIN):
        for g in range(GROUPS):
            at = w * GROUPS + g
            notes = jnp.where(lane == at, p_cols[g, w].astype(jnp.float32), notes)
            for m in range(KEPT):
                value = square_cols[g, m, w].astype(jnp.float32)
                notes = jnp.where(lane == WIN * GROUPS + at * KEPT + m, value, notes)
    notes = notes.astype(jnp.bfloat16)
    marks = jnp.zeros((2 * 8, BS), jnp.float32)
    for g in range(GROUPS):
        for k in range(BR):
            marks = jnp.where(lane == g * BR + k, p_cols[g, k].astype(jnp.float32), marks)

    group = lax.broadcasted_iota(jnp.int32, (BS, BS), 1) // Q
    first.wait()
    for p in range(WIN // 2):
        tile = jnp.zeros((BS, BS), jnp.float32)
        for i in range(2 * GROUPS):
            part = heads[2 * p + i // GROUPS, i % GROUPS].astype(jnp.float32)
            moved = pltpu.roll(part, lax.rem((i - rep) * Q + BS, BS), 1)
            tile = jnp.where(group == i, moved, tile)
        tile = tile.astype(jnp.bfloat16)
        for c in range(COLS):
            spread[c, p * BS : (p + 1) * BS, :] = tile
    for c in range(COLS):
        spread[c, WIN // 2 * BS :, :] = notes

    second.wait()
    peak = jnp.zeros((Q, BS), jnp.float32)
    for k in range(BR):
        for g in range(GROUPS):
            peak = jnp.maximum(peak, jnp.abs(shares[k, g].astype(jnp.float32)))
    peak = jnp.maximum(jnp.max(peak, axis=(0, 1), keepdims=True), 1e-37)
    power = jnp.clip(13.0 - jnp.floor(jnp.log2(peak)), 0.0, 110.0)
    scale = jnp.exp2(power)
    for k in range(BR):
        for g in range(GROUPS):
            block = shares[k, g].astype(jnp.float32) * scale
            panel[k * PAIR + g * Q : k * PAIR + (g + 1) * Q, :] = block.astype(jnp.bfloat16)
    marks = jnp.where(lane == MARKS, power, marks)
    panel[BR * PAIR :, :] = marks.astype(jnp.bfloat16)


def square_kernel(notes_in, marks_in, keep_in, lefts, panels, out, right, held, sems, *small):
    notes, marks, keep, small_sems = small
    waits = scalars((notes_in, marks_in, keep_in), small[:-1], small_sems)

    def pick(p):
        for half in range(2):
            for s in range(ROWS):
                k = notes[s // GROUPS, 0, (2 * p + half) * GROUPS + s % GROUPS]
                rows = pl.ds(pl.multiple_of(k * PAIR, PAIR), PAIR)
                pltpu.make_async_copy(
                    panels.at[s, rows, :], held.at[p, half, s], sems.at[p]
                ).start()

    waits[0].wait()
    pick(0)
    group = lax.broadcasted_iota(jnp.int32, (BS, BS), 1) // Q
    right[...] = jnp.zeros_like(right)
    for copy in waits[1:]:
        copy.wait()

    def pair(p, _):
        if p < WIN // 2 - 1:
            pick(p + 1)

        pltpu.make_async_copy(held.at[p], held.at[p], sems.at[p]).wait()
        rows = pl.ds(pl.multiple_of(p * BS, BS), BS)
        left = jnp.concatenate([lefts[c, rows, :] for c in range(COLS)], axis=1)
        for half in range(2):
            w = 2 * p + half
            for s in range(ROWS):
                k = notes[s // GROUPS, 0, w * GROUPS + s % GROUPS]
                at = (s // GROUPS) * BS + (half * GROUPS + s % GROUPS) * Q
                for g in range(GROUPS):
                    block = held[p, half, s, g * Q : (g + 1) * Q, :]
                    col = marks[s, g * BR + k]
                    for m in range(KEPT):
                        n = (g * KEPT + m) * BS
                        right[half, at : at + Q, n : n + BS] = jnp.where(
                            col == keep[g, m, w], block, jnp.zeros_like(block)
                        )
            full = jnp.dot(left, right[half], preferred_element_type=jnp.float32)
            p4 = [full[:, i * BS : (i + 1) * BS] for i in range(SLOTS)]
            u = [jnp.where(group < 2, p4[i], pltpu.roll(p4[i + 2], BS // 2, 1)) for i in range(2)]
            u += [jnp.where(group < 2, pltpu.roll(p4[i], BS // 2, 1), p4[i + 2]) for i in range(2)]
            for i in (0, 2):
                one = jnp.where(group % 2 == 0, u[i], pltpu.roll(u[i + 1], Q, 1))
                two = jnp.where(group % 2 == 0, pltpu.roll(u[i], BS - Q, 1), u[i + 1])
                out[i, w] = one.astype(jnp.bfloat16)
                out[i + 1, w] = two.astype(jnp.bfloat16)
        return 0

    for p in range(WIN // 2):
        pair(p, 0)


def layout_kernel(notes_in, marks_in, keep_in, cube_keep_in, panels, right, held, sems, *small):
    notes, marks, keep, cube_keep, small_sems = small
    sources = (notes_in, marks_in, keep_in, cube_keep_in)
    waits = scalars(sources, small[:-1], small_sems)
    copies = fetch(panels, held, sems)
    clear(right, INNER)
    for copy in waits:
        copy.wait()
    rep = lax.axis_index("rep")
    wide = lax.broadcasted_iota(jnp.int32, (BS, BS), 1)
    tall = lax.broadcasted_iota(jnp.int32, (BS, BS), 0)
    place = wide == (rep * Q + tall % Q)

    def own(w, _):
        for g in range(GROUPS):
            found = jnp.zeros((BS, BS), jnp.float32)
            for m in range(KEPT):
                scale = jnp.where(keep[g, m, w] == cube_keep[g, 0, w], -1.5, 0.0)
                found = jnp.where(tall // Q == g * KEPT + m, scale, found)
            found = jnp.where(place, found, 0.0).astype(jnp.bfloat16)
            right[w, INNER : INNER + BS, g * BS : (g + 1) * BS] = found
        return 0

    lax.fori_loop(0, WIN, own, 0)
    for s in range(ROWS):
        copies[s].wait()
        for w in range(WIN):
            for t in range(KEPT):
                at = WIN * GROUPS + (w * GROUPS + s % GROUPS) * KEPT + t
                k = notes[s // GROUPS, 0, at]
                for g in range(GROUPS):
                    hit = marks[s, g * BR + k] == cube_keep[g, 0, w]
                    row = (s * KEPT + t) * Q
                    block = held[s, pl.ds(pl.multiple_of(k * PAIR + g * Q, Q), Q), :]
                    put(right, w, row, g, block, hit, INNER + BS)


def cube_kernel(own, same, other, right, out):
    first = lax.rem(lax.axis_index("col"), 2) == 0
    for w in range(WIN):
        tiles = []
        for y in range(CHIPS):
            one, two = same[y, w], other[y, w]
            tiles += [jnp.where(first, one, two), jnp.where(first, two, one)]
        left = jnp.concatenate(tiles + [own[w]], axis=1)
        total = jnp.dot(left, right[w, : INNER + BS, :], preferred_element_type=jnp.float32)
        total = -2.0 * total
        for g in range(GROUPS):
            out[w, g] = total[:, g * BS : (g + 1) * BS].astype(jnp.bfloat16)


def small_room(*arrays):
    held = [pltpu.SMEM(a.shape, a.dtype) for a in arrays]
    return (*held, pltpu.SemaphoreType.DMA((len(arrays),)))


def shaped(*shape):
    return jax.ShapeDtypeStruct(shape, jnp.bfloat16)


def call(kernel, out, scalars, arrays, scratch=(), specs=None, room=8, work=(0, 0)):
    return pl.pallas_call(
        kernel,
        out_shape=out,
        in_specs=[SMEM] * len(scalars) + (specs or [VMEM] * len(arrays)),
        out_specs=jax.tree.map(lambda _: VMEM, out),
        scratch_shapes=scratch,
        cost_estimate=pl.CostEstimate(flops=work[0], bytes_accessed=work[1], transcendentals=0),
        compiler_params=pltpu.CompilerParams(vmem_limit_bytes=room * 2**20),
    )(*scalars, *arrays)


def on_device(p_vals, p_cols, square_cols, cube_cols):
    own_cols = p_cols.T
    keep = square_cols.transpose(1, 2, 0)
    cube_keep = cube_cols.transpose(1, 2, 0)

    spread, panel = call(
        prepare_kernel,
        (shaped(COLS, WIN // 2 * BS + 16, BS), shaped(TALL, BS)),
        (),
        [own_cols, keep, p_vals],
        [
            pltpu.VMEM((WIN, GROUPS, BS, BS), jnp.bfloat16),
            pltpu.VMEM((BR, GROUPS, Q, BS), jnp.bfloat16),
            pltpu.SemaphoreType.DMA((2,)),
            *small_room(own_cols, keep),
        ],
        [HBM] * 3,
        63,
    )
    lefts = lax.all_to_all(spread, "col", 0, 0)
    panels = lax.all_gather(panel.astype(jnp.float16), "row")
    panels = lax.optimization_barrier(panels)
    notes = lefts[:, WIN // 2 * BS : WIN // 2 * BS + 1, :].astype(jnp.int32)
    marks = panels[:, BR * PAIR, :].astype(jnp.float32)
    back = jnp.exp2(-marks[:, MARKS])[:, None, None]
    marks = marks.astype(jnp.int32)
    panels = (panels.astype(jnp.float32) * back).astype(jnp.bfloat16)

    partial = call(
        square_kernel,
        shaped(REPS, WIN, BS, BS),
        (),
        (notes, marks, keep, lefts, panels),
        [
            pltpu.VMEM((2, COLS * BS, SLOTS * BS), jnp.bfloat16),
            pltpu.VMEM((WIN // 2, 2, ROWS, PAIR, BS), jnp.bfloat16),
            pltpu.SemaphoreType.DMA((WIN // 2,)),
            *small_room(notes, marks, keep),
        ],
        [HBM] * 3 + [VMEM, HBM],
        ROOM,
        (WIN * 2 * BS * ROWS * Q * SLOTS * BS, panels.size * 2),
    )
    right = call(
        layout_kernel,
        shaped(WIN, INNER + BS + Q, GROUPS * BS),
        (),
        [notes, marks, keep, cube_keep, panels],
        [
            pltpu.VMEM(panels.shape, panels.dtype),
            pltpu.SemaphoreType.DMA((ROWS,)),
            *small_room(notes, marks, keep, cube_keep),
        ],
        [HBM] * 5,
        ROOM,
        (0, 3 * panels.size * 2),
    )
    parts = lax.all_to_all(partial, "rep", 0, 0, tiled=True)
    own = jnp.sum(parts.astype(jnp.float32), axis=0).astype(jnp.bfloat16)
    same = lax.all_to_all(
        jnp.broadcast_to(own[None], (CHIPS,) + own.shape), "col", 0, 0, axis_index_groups=SAME_CORE
    )
    other = lax.ppermute(same, "col", CORES)
    partial = call(
        cube_kernel,
        shaped(WIN, GROUPS, BS, BS),
        (),
        (own, same, other, right),
        work=(WIN * 2 * BS * (INNER + BS) * GROUPS * BS, right.size * 2),
    )
    parts = lax.all_to_all(partial, "rep", 0, 0, tiled=True)
    parts = parts.reshape((REPS, WIN // REPS) + parts.shape[1:]).astype(jnp.float32)
    return jnp.sum(parts, axis=0).astype(jnp.bfloat16)[:, :, None]


def solution(mesh):
    in_specs = (
        P("row", "col", None, None),
        P("row", "col"),
        P("row", "col", None),
        P("row", "col", None),
    )
    out_specs = P(("row", "rep"), "col", None, None, None)
    return jax.shard_map(
        on_device, mesh=mesh, in_specs=in_specs, out_specs=out_specs, check_vma=False
    )
```

```python
import jax
import jax.numpy as jnp
from jax import lax
from jax.experimental import pallas as pl
from jax.experimental.pallas import tpu as pltpu
from jax.sharding import PartitionSpec as P

ROWS = 16
COLS = 8
CHIPS = 4
REPS = 4
GROUPS = 2
WIN = 8
BR = 24
BS = 128
Q = BS // REPS
KEPT = 2
SLOTS = GROUPS * KEPT
MARKS = GROUPS * BR
ROOM = 48
INNER = ROWS * KEPT * Q
PAIR = GROUPS * Q
TALL = BR * PAIR + 16

CORES = [(i, i ^ 1) for i in range(COLS)]
SAME_CORE = [[c + i for i in range(0, COLS, 2)] for c in range(2)]

SMEM = pl.BlockSpec(memory_space=pltpu.SMEM)
HBM = pl.BlockSpec(memory_space=pltpu.HBM)
VMEM = pl.BlockSpec(memory_space=pltpu.VMEM)


def put(right, w, row, lane_tile, block, hit, spare):
    row = pl.multiple_of(jnp.where(hit, row, spare), Q)
    right[w, pl.ds(row, Q), pl.ds(pl.multiple_of(lane_tile * BS, BS), BS)] = block


def clear(right, rows):
    def one(w, _):
        right[w, :rows, :] = jnp.zeros((rows, right.shape[2]), right.dtype)
        return 0

    lax.fori_loop(0, WIN, one, 0)


def scalars(sources, held, sems):
    copies = [pltpu.make_async_copy(*pair, sems.at[i]) for i, pair in enumerate(zip(sources, held))]
    for copy in copies:
        copy.start()
    return copies


def fetch(panels, held, sems):
    copies = [pltpu.make_async_copy(panels.at[s], held.at[s], sems.at[s]) for s in range(ROWS)]
    for copy in copies:
        copy.start()
    return copies


def prepare_kernel(p_cols_in, square_in, p_vals, spread, panel, heads, shares, sems, *small):
    p_cols, square_cols, small_sems = small
    rep = lax.axis_index("rep")
    rows = pl.ds(pl.multiple_of(rep * Q, Q), Q)
    first = pltpu.make_async_copy(p_vals.at[:WIN], heads, sems.at[0])
    second = pltpu.make_async_copy(p_vals.at[:, :, rows, :], shares, sems.at[1])
    first.start()
    second.start()
    for copy in scalars((p_cols_in, square_in), (p_cols, square_cols), small_sems):
        copy.wait()
    lane = lax.broadcasted_iota(jnp.int32, (2 * 8, BS), 1)
    notes = jnp.zeros((2 * 8, BS), jnp.float32)
    for w in range(WIN):
        for g in range(GROUPS):
            at = w * GROUPS + g
            notes = jnp.where(lane == at, p_cols[g, w].astype(jnp.float32), notes)
            for m in range(KEPT):
                value = square_cols[g, m, w].astype(jnp.float32)
                notes = jnp.where(lane == WIN * GROUPS + at * KEPT + m, value, notes)
    notes = notes.astype(jnp.bfloat16)
    marks = jnp.zeros((2 * 8, BS), jnp.float32)
    for g in range(GROUPS):
        for k in range(BR):
            marks = jnp.where(lane == g * BR + k, p_cols[g, k].astype(jnp.float32), marks)

    group = lax.broadcasted_iota(jnp.int32, (BS, BS), 1) // Q
    first.wait()
    for p in range(WIN // 2):
        tile = jnp.zeros((BS, BS), jnp.float32)
        for i in range(2 * GROUPS):
            part = heads[2 * p + i // GROUPS, i % GROUPS].astype(jnp.float32)
            moved = pltpu.roll(part, lax.rem((i - rep) * Q + BS, BS), 1)
            tile = jnp.where(group == i, moved, tile)
        tile = tile.astype(jnp.bfloat16)
        for c in range(COLS):
            spread[c, p * BS : (p + 1) * BS, :] = tile
    for c in range(COLS):
        spread[c, WIN // 2 * BS :, :] = notes

    second.wait()
    peak = jnp.zeros((Q, BS), jnp.float32)
    for k in range(BR):
        for g in range(GROUPS):
            peak = jnp.maximum(peak, jnp.abs(shares[k, g].astype(jnp.float32)))
    peak = jnp.maximum(jnp.max(peak, axis=(0, 1), keepdims=True), 1e-37)
    power = jnp.clip(13.0 - jnp.floor(jnp.log2(peak)), 0.0, 110.0)
    scale = jnp.exp2(power)
    for k in range(BR):
        for g in range(GROUPS):
            block = shares[k, g].astype(jnp.float32) * scale
            panel[k * PAIR + g * Q : k * PAIR + (g + 1) * Q, :] = block.astype(jnp.bfloat16)
    marks = jnp.where(lane == MARKS, power, marks)
    panel[BR * PAIR :, :] = marks.astype(jnp.bfloat16)


def square_kernel(notes_in, marks_in, keep_in, lefts, panels, out, right, held, sems, *small):
    notes, marks, keep, small_sems = small
    waits = scalars((notes_in, marks_in, keep_in), small[:-1], small_sems)

    def pick(p):
        for half in range(2):
            for s in range(ROWS):
                k = notes[s // GROUPS, 0, (2 * p + half) * GROUPS + s % GROUPS]
                rows = pl.ds(pl.multiple_of(k * PAIR, PAIR), PAIR)
                pltpu.make_async_copy(
                    panels.at[s, rows, :], held.at[p, half, s], sems.at[p]
                ).start()

    waits[0].wait()
    pick(0)
    group = lax.broadcasted_iota(jnp.int32, (BS, BS), 1) // Q
    right[...] = jnp.zeros_like(right)
    for copy in waits[1:]:
        copy.wait()

    def pair(p, _):
        if p < WIN // 2 - 1:
            pick(p + 1)

        pltpu.make_async_copy(held.at[p], held.at[p], sems.at[p]).wait()
        rows = pl.ds(pl.multiple_of(p * BS, BS), BS)
        left = jnp.concatenate([lefts[c, rows, :] for c in range(COLS)], axis=1)
        for half in range(2):
            w = 2 * p + half
            for s in range(ROWS):
                k = notes[s // GROUPS, 0, w * GROUPS + s % GROUPS]
                at = (s // GROUPS) * BS + (half * GROUPS + s % GROUPS) * Q
                for g in range(GROUPS):
                    block = held[p, half, s, g * Q : (g + 1) * Q, :]
                    col = marks[s, g * BR + k]
                    for m in range(KEPT):
                        n = (g * KEPT + m) * BS
                        right[half, at : at + Q, n : n + BS] = jnp.where(
                            col == keep[g, m, w], block, jnp.zeros_like(block)
                        )
            full = jnp.dot(left, right[half], preferred_element_type=jnp.float32)
            p4 = [full[:, i * BS : (i + 1) * BS].astype(jnp.bfloat16) for i in range(SLOTS)]
            u = [jnp.where(group < 2, p4[i], pltpu.roll(p4[i + 2], BS // 2, 1)) for i in range(2)]
            u += [jnp.where(group < 2, pltpu.roll(p4[i], BS // 2, 1), p4[i + 2]) for i in range(2)]
            for i in (0, 2):
                one = jnp.where(group % 2 == 0, u[i], pltpu.roll(u[i + 1], Q, 1))
                two = jnp.where(group % 2 == 0, pltpu.roll(u[i], BS - Q, 1), u[i + 1])
                out[i, w] = one
                out[i + 1, w] = two
        return 0

    for p in range(WIN // 2):
        pair(p, 0)


def layout_kernel(notes_in, marks_in, keep_in, cube_keep_in, panels, right, held, sems, *small):
    notes, marks, keep, cube_keep, small_sems = small
    sources = (notes_in, marks_in, keep_in, cube_keep_in)
    waits = scalars(sources, small[:-1], small_sems)
    copies = fetch(panels, held, sems)
    clear(right, INNER)
    for copy in waits:
        copy.wait()
    rep = lax.axis_index("rep")
    wide = lax.broadcasted_iota(jnp.int32, (BS, BS), 1)
    tall = lax.broadcasted_iota(jnp.int32, (BS, BS), 0)
    place = wide == (rep * Q + tall % Q)

    def own(w, _):
        for g in range(GROUPS):
            found = jnp.zeros((BS, BS), jnp.float32)
            for m in range(KEPT):
                scale = jnp.where(keep[g, m, w] == cube_keep[g, 0, w], -1.5, 0.0)
                found = jnp.where(tall // Q == g * KEPT + m, scale, found)
            found = jnp.where(place, found, 0.0).astype(jnp.bfloat16)
            right[w, INNER : INNER + BS, g * BS : (g + 1) * BS] = found
        return 0

    lax.fori_loop(0, WIN, own, 0)
    for s in range(ROWS):
        copies[s].wait()
        for w in range(WIN):
            for t in range(KEPT):
                at = WIN * GROUPS + (w * GROUPS + s % GROUPS) * KEPT + t
                k = notes[s // GROUPS, 0, at]
                for g in range(GROUPS):
                    hit = marks[s, g * BR + k] == cube_keep[g, 0, w]
                    row = (s * KEPT + t) * Q
                    block = held[s, pl.ds(pl.multiple_of(k * PAIR + g * Q, Q), Q), :]
                    put(right, w, row, g, block, hit, INNER + BS)


def cube_kernel(own, same, other, right, out):
    first = lax.rem(lax.axis_index("col"), 2) == 0
    for w in range(WIN):
        tiles = []
        for y in range(CHIPS):
            one, two = same[y, w], other[y, w]
            tiles += [jnp.where(first, one, two), jnp.where(first, two, one)]
        left = jnp.concatenate(tiles + [own[w]], axis=1)
        total = jnp.dot(left, right[w, : INNER + BS, :], preferred_element_type=jnp.float32)
        total = -2.0 * total
        for g in range(GROUPS):
            out[w, g] = total[:, g * BS : (g + 1) * BS].astype(jnp.bfloat16)


def small_room(*arrays):
    held = [pltpu.SMEM(a.shape, a.dtype) for a in arrays]
    return (*held, pltpu.SemaphoreType.DMA((len(arrays),)))


def shaped(*shape):
    return jax.ShapeDtypeStruct(shape, jnp.bfloat16)


def call(kernel, out, scalars, arrays, scratch=(), specs=None, room=8, work=(0, 0)):
    return pl.pallas_call(
        kernel,
        out_shape=out,
        in_specs=[SMEM] * len(scalars) + (specs or [VMEM] * len(arrays)),
        out_specs=jax.tree.map(lambda _: VMEM, out),
        scratch_shapes=scratch,
        cost_estimate=pl.CostEstimate(flops=work[0], bytes_accessed=work[1], transcendentals=0),
        compiler_params=pltpu.CompilerParams(vmem_limit_bytes=room * 2**20),
    )(*scalars, *arrays)


def on_device(p_vals, p_cols, square_cols, cube_cols):
    own_cols = p_cols.T
    keep = square_cols.transpose(1, 2, 0)
    cube_keep = cube_cols.transpose(1, 2, 0)

    spread, panel = call(
        prepare_kernel,
        (shaped(COLS, WIN // 2 * BS + 16, BS), shaped(TALL, BS)),
        (),
        [own_cols, keep, p_vals],
        [
            pltpu.VMEM((WIN, GROUPS, BS, BS), jnp.bfloat16),
            pltpu.VMEM((BR, GROUPS, Q, BS), jnp.bfloat16),
            pltpu.SemaphoreType.DMA((2,)),
            *small_room(own_cols, keep),
        ],
        [HBM] * 3,
        63,
    )
    lefts = lax.all_to_all(spread, "col", 0, 0)
    panels = lax.all_gather(panel.astype(jnp.float16), "row")
    panels = lax.optimization_barrier(panels)
    notes = lefts[:, WIN // 2 * BS : WIN // 2 * BS + 1, :].astype(jnp.int32)
    marks = panels[:, BR * PAIR, :].astype(jnp.float32)
    back = jnp.exp2(-marks[:, MARKS])[:, None, None]
    marks = marks.astype(jnp.int32)
    panels = (panels.astype(jnp.float32) * back).astype(jnp.bfloat16)

    partial = call(
        square_kernel,
        shaped(REPS, WIN, BS, BS),
        (),
        (notes, marks, keep, lefts, panels),
        [
            pltpu.VMEM((2, COLS * BS, SLOTS * BS), jnp.bfloat16),
            pltpu.VMEM((WIN // 2, 2, ROWS, PAIR, BS), jnp.bfloat16),
            pltpu.SemaphoreType.DMA((WIN // 2,)),
            *small_room(notes, marks, keep),
        ],
        [HBM] * 3 + [VMEM, HBM],
        ROOM,
        (WIN * 2 * BS * ROWS * Q * SLOTS * BS, panels.size * 2),
    )
    right = call(
        layout_kernel,
        shaped(WIN, INNER + BS + Q, GROUPS * BS),
        (),
        [notes, marks, keep, cube_keep, panels],
        [
            pltpu.VMEM(panels.shape, panels.dtype),
            pltpu.SemaphoreType.DMA((ROWS,)),
            *small_room(notes, marks, keep, cube_keep),
        ],
        [HBM] * 5,
        ROOM,
        (0, 3 * panels.size * 2),
    )
    parts = lax.all_to_all(partial, "rep", 0, 0, tiled=True)
    own = jnp.sum(parts.astype(jnp.float32), axis=0).astype(jnp.bfloat16)
    same = lax.all_to_all(
        jnp.broadcast_to(own[None], (CHIPS,) + own.shape), "col", 0, 0, axis_index_groups=SAME_CORE
    )
    other = lax.ppermute(same, "col", CORES)
    partial = call(
        cube_kernel,
        shaped(WIN, GROUPS, BS, BS),
        (),
        (own, same, other, right),
        work=(WIN * 2 * BS * (INNER + BS) * GROUPS * BS, right.size * 2),
    )
    parts = lax.all_to_all(partial, "rep", 0, 0, tiled=True)
    parts = parts.reshape((REPS, WIN // REPS) + parts.shape[1:]).astype(jnp.float32)
    return jnp.sum(parts, axis=0).astype(jnp.bfloat16)[:, :, None]


def solution(mesh):
    in_specs = (
        P("row", "col", None, None),
        P("row", "col"),
        P("row", "col", None),
        P("row", "col", None),
    )
    out_specs = P(("row", "rep"), "col", None, None, None)
    return jax.shard_map(
        on_device, mesh=mesh, in_specs=in_specs, out_specs=out_specs, check_vma=False
    )
```
